512 devices in a mesh: segment: 8 (over x, core), seq: 64 (over z, y).
Axes of the slice: x: 4, y: 4, z: 16, core: 2. Of those that a mesh axis runs over, the one named last changes fastest.
Arguments:
- cotangent: bfloat16 [8, 8192, 4096], P('segment', 'seq'), may hold values from -6 to 6
- gates: bfloat16 [8, 2, 8192, 4096], P('segment', None, 'seq'), may hold values from -6 to 6
- short_weight: float32 [8, 2, 7, 4096], P('segment'), may hold values from -1 to 1
- decay_rates: float32 [8, 2, 4096, 16], P('segment', None, 'seq'), may hold values from 3.6621094e-05 to 0.0333333333
- residues: float32 [8, 2, 4096, 16], P('segment', None, 'seq'), may hold values from -1 to 1
Outputs:
- grad_out: bfloat16 [8, 8192, 4096], P('segment', 'seq')
The draws below stay inside these ranges and needn't reach their ends.
All inputs are finite; a program needn't handle non-finite values.
Results may differ from the reference program's by a relative error of at most 0.0061.
Values may be sent and summed in bfloat16 or wider, within the bound.
No kernel may reach another device: no remote copies, remote signals or barrier semaphores. Data moves between devices by JAX's collectives and lax.ppermute only.
A program may use at most 128 MiB of HBM per device.

```python
import math
import jax
import jax.numpy as jnp
from jax import lax

C = 4096
STEPS = 2
MODES = 16
SHORT = 7
SEGMENTS = 8
LENGTH = 8192


def mode_pair(key):
    folded = jax.random.fold_in(key, 11)
    key_rates, second = jax.random.split(folded)
    array_shape = (SEGMENTS, STEPS, C, MODES)
    spread = jax.random.uniform(key_rates, array_shape, jnp.float32)
    lowest = 0.3 / LENGTH
    highest = 1.0 / 30.0
    decay_values = jnp.exp(math.log(lowest) + spread * (math.log(highest) - math.log(lowest)))
    normal_part = jnp.clip(jax.random.normal(second, array_shape, jnp.float32), -3.0, 3.0)
    residue_values = normal_part * 0.4 * jnp.sqrt(2.0 * decay_values)
    return (decay_values, residue_values)


def draw_decay_rates(key, part):
    return mode_pair(key)[0]


def draw_residues(key, part):
    return mode_pair(key)[1]


def levels(own_key, shape, cuts, least, top_value):
    def one(position, shards_of):
        steps = jax.random.uniform(jax.random.fold_in(jax.random.fold_in(own_key, 6), position), (shards_of,), jnp.float32, least / len(cuts), top_value / len(cuts))
        return jnp.repeat(jnp.exp(steps), shape[position] // shards_of).reshape((-1,) + (1,) * (len(shape) - position - 1))

    loudness = one(*cuts[0])
    for cut in cuts[1:]:
        loudness = loudness * one(*cut)
    return loudness


def noise(stream_key, shape, deviation, limit, shards=(), kind=jnp.bfloat16):
    drawn = jax.random.normal(stream_key, shape, jnp.float32) * deviation
    if len(shards) > 0:
        drawn = levels(stream_key, shape, shards, -0.22, 0.18) * drawn
    return jnp.clip(drawn, min=-limit, max=limit).astype(kind)


def setup_inputs(seed: int = 0) -> dict:
    seeds = jax.random.split(jax.random.key(seed), 6)
    return {
        "cotangent": noise(seeds[0], (SEGMENTS, LENGTH, C), 1.0, 6.0, ((0, 8), (1, 64))),
        "gates": noise(seeds[1], (SEGMENTS, STEPS, LENGTH, C), 1.0, 6.0, ((0, 8), (2, 64))),
        "short_weight": noise(seeds[2], (SEGMENTS, STEPS, SHORT, C), 0.2, 1.0, ((0, 8),), jnp.float32),
        "decay_rates": draw_decay_rates(jax.random.fold_in(seeds[5], 71), 0),
        "residues": draw_residues(jax.random.fold_in(seeds[5], 71), 0),
    }


def filter_corr(values, rate_block, weight_block):
    extent = values.shape[1]
    places = jnp.arange(extent).astype(jnp.float32)
    filter_taps = jnp.sum(weight_block[:, None, :] * jnp.exp(-rate_block[:, None, :] * places[None, :, None]), axis=-1)
    spec_filter = jnp.fft.fft(filter_taps, n=2 * extent, axis=-1)
    spec_values = jnp.fft.fft(values, n=2 * extent, axis=-1)
    joined = jnp.fft.ifft(spec_values * jnp.conj(spec_filter), axis=-1)
    return jnp.real(joined)[:, :extent].astype(jnp.float32)


def layer_back(gradient, gate, weight, rates_here, weights_here):
    product = (gate.astype(jnp.float32) * gradient.astype(jnp.float32)).astype(jnp.bfloat16)
    product_wide = lax.optimization_barrier(product).astype(jnp.float32)
    block = math.gcd(C, 64)
    blocks_count = C // block
    blocks = product_wide.T.reshape(blocks_count, block, LENGTH)
    carried = lax.map(lambda parts: filter_corr(parts[0], parts[1], parts[2]),
                      (blocks, rates_here.reshape(blocks_count, block, MODES), weights_here.reshape(blocks_count, block, MODES)))
    carried = carried.reshape(C, LENGTH).T.astype(jnp.bfloat16)
    carried_wide = lax.optimization_barrier(carried).astype(jnp.float32)
    extended = jnp.concatenate([carried_wide, jnp.zeros((SHORT - 1, C), jnp.float32)], axis=0)
    tail_sum = jnp.zeros((LENGTH, C), jnp.float32)
    for offset in range(SHORT):
        tail_sum = tail_sum + weight[offset][None, :] * extended[offset:offset + LENGTH]
    return (gradient.astype(jnp.float32) + tail_sum).astype(jnp.bfloat16)


def reference(cotangent, gates, short_weight, decay_rates, residues):
    gradients = cotangent
    for layer_index in range(STEPS):
        updated = lax.map(lambda parts: layer_back(parts[0], parts[1], parts[2], parts[3], parts[4]),
                          (gradients, gates[:, layer_index], short_weight[:, layer_index], decay_rates[:, layer_index], residues[:, layer_index]))
        gradients = jnp.roll(updated, -1, axis=0)
    return gradients
```

```python
import jax
import jax.numpy as jnp
import numpy as np
from jax import lax
from jax.experimental import pallas as pl
from jax.experimental.pallas import tpu as pltpu
from jax.sharding import PartitionSpec as P

STEPS = 2
SHORT = 7
NODES = 12
HALF = NODES // 2
TILE = 512
BF = jnp.bfloat16
F32 = jnp.float32


def cheb(low, high):
    k = np.arange(NODES)
    x = np.cos(np.pi * (2 * k + 1) / (2 * NODES))
    return 0.5 * (low + high) + 0.5 * (high - low) * x


def lagrange(nodes, points):
    points = np.asarray(points, np.float64)
    out = np.ones((len(nodes),) + points.shape)
    for n in range(len(nodes)):
        for k in range(len(nodes)):
            if k != n:
                out[n] *= (points - nodes[k]) / (nodes[n] - nodes[k])
    return out


def split_pair(matrix):
    high = matrix.astype(jnp.bfloat16)
    low = (matrix - high.astype(np.float64)).astype(jnp.bfloat16)
    return np.concatenate([high, low], axis=1)


def packed_rows(values):
    out = np.zeros((8, 128), np.float32)
    out[:HALF, :64] = values[:HALF, None]
    out[:HALF, 64:] = values[HALF:, None]
    return out


def constants(rows):
    source = cheb(0.0, rows - 1.0)
    target = cheb(0.0, rows + SHORT - 2.0)
    lags = cheb(2.0 - SHORT, rows - 1.0)
    moment = np.zeros((16, rows))
    basis = lagrange(source, np.arange(rows))
    moment[:HALF] = basis[:HALF]
    moment[8 : 8 + HALF] = basis[HALF:]
    spread = np.zeros((rows + 8, 16))
    basis = lagrange(target, np.arange(rows + SHORT - 1)).T
    spread[: rows + SHORT - 1, :HALF] = basis[:, :HALF]
    spread[: rows + SHORT - 1, 8 : 8 + HALF] = basis[:, HALF:]
    place = np.arange(rows)
    lag = place[None, :] - place[:, None]
    inside = lagrange(lags, lag) * (lag >= 0)[None]
    place = np.arange(16)
    lag = place[None, :] - place[:8, None]
    live = (lag < 0) & (place[:8, None] < SHORT - 1)
    beyond = -lagrange(lags, np.where(live, lag, 0)) * live[None]
    return dict(
        source=source,
        moment=split_pair(moment),
        spread=split_pair(spread),
        inside=split_pair(inside.reshape(NODES * rows, rows)),
        beyond=split_pair(beyond.reshape(NODES * 8, 16)),
        target_gap=packed_rows(rows - target),
        lag_nodes=packed_rows(lags),
    )


def doubled(x):
    return jnp.concatenate([x, x], axis=1)


def low_lanes():
    return lax.broadcasted_iota(jnp.int32, (8, 128), 1) < 64


def unpack(blocks, low):
    first, second = blocks
    return (
        jnp.where(low, first, pltpu.roll(second, 64, 1)),
        jnp.where(low, pltpu.roll(first, 64, 1), second),
    )


def moments_kernel(g_ref, gate_ref, moment_ref, lag_ref, rate_ref, res_ref, pay_ref, halo_ref, taps_ref):
    low = low_lanes()

    @pl.when(pl.program_id(0) == 0)
    def _():
        rate = doubled(rate_ref[0])
        res = doubled(res_ref[0])
        total = jnp.zeros((8, 128), F32)
        for m in range(rate.shape[0]):
            total = total + res[m : m + 1] * jnp.exp(-rate[m : m + 1] * lag_ref[...])
        taps_ref[...] = total

    product = (gate_ref[0].astype(F32) * g_ref[...].astype(F32)).astype(BF)
    halo_ref[...] = product[:16]
    moments = jnp.dot(moment_ref[...], jnp.concatenate([product, product], axis=0), preferred_element_type=F32)
    taps = taps_ref[...]
    for t in range(product.shape[1] // 128):
        pair = moments[0:8, t * 128 : t * 128 + 128], moments[8:16, t * 128 : t * 128 + 128]
        first, second = unpack(pair, low)
        pay_ref[t * 32 : t * 32 + 16, :] = jnp.concatenate([first, taps], axis=0).astype(BF)
        pay_ref[t * 32 + 16 : t * 32 + 32, :] = jnp.concatenate([second, taps], axis=0).astype(BF)


def scan_kernel(source, rows, shards, pay_ref, rate_ref, res_ref, gap_ref, out_ref):
    low = low_lanes()
    rate = doubled(rate_ref[0])
    res = doubled(res_ref[0])
    enter = []
    for r in range(HALF):
        place = jnp.where(low, F32(source[r]), F32(source[r + HALF]))
        enter.append([jnp.exp(-rate[8 * o : 8 * o + 8] * place) for o in range(2)])
    step = [jnp.exp(-rate[8 * o : 8 * o + 8] * F32(rows)) for o in range(2)]
    leave = [res[m : m + 1] * jnp.exp(-rate[m : m + 1] * gap_ref[...]) for m in range(16)]

    def one(shard, state):
        total = jnp.zeros((8, 128), F32)
        for m in range(16):
            total = total + leave[m] * state[m // 8][m % 8 : m % 8 + 1]
        block = pay_ref[pl.ds(pl.multiple_of(shard * 16, 16), 16), :].astype(F32)
        sums = [None, None]
        for o in range(2):
            part = enter[0][o] * block[0:1]
            for r in range(1, HALF):
                part = part + enter[r][o] * block[r : r + 1]
            sums[o] = part + pltpu.roll(part, 64, 1)
        return total, tuple(step[o] * state[o] + sums[o] for o in range(2))

    def pair(i, state):
        index = shards // 2 - 1 - i
        later, state = one(2 * index + 1, state)
        earlier, state = one(2 * index, state)
        out_ref[pl.ds(pl.multiple_of(index * 16, 16), 16), :] = jnp.concatenate([earlier, later], axis=0).astype(BF)
        return state

    zero = jnp.zeros((8, 128), F32)
    lax.fori_loop(0, shards // 2, pair, (zero, zero), unroll=2)


def inside_kernel(g_ref, gate_ref, halo_ref, pay_ref, inside_ref, beyond_ref, local_ref, rim_ref):
    rows, width = g_ref.shape
    low = low_lanes()
    product = (gate_ref[0].astype(F32) * g_ref[...].astype(F32)).astype(BF)
    parts = []
    for t in range(width // 128):
        blocks = [pay_ref[t * 32 + 16 * k : t * 32 + 16 * k + 16, :].astype(F32)[8:16] for k in range(2)]
        parts.append(unpack(blocks, low))
    taps = [jnp.concatenate([part[h] for part in parts], axis=1) for h in range(2)]
    waves = jnp.dot(inside_ref[...], jnp.concatenate([product, product], axis=0), preferred_element_type=F32)
    halo = halo_ref[...]
    edges = jnp.dot(beyond_ref[...], jnp.concatenate([halo, halo], axis=0), preferred_element_type=F32)
    local = None
    rim = None
    for n in range(NODES):
        tap = taps[n // HALF][n % HALF : n % HALF + 1]
        wave = tap * waves[n * rows : (n + 1) * rows]
        edge = tap * edges[n * 8 : (n + 1) * 8]
        local = wave if local is None else local + wave
        rim = edge if rim is None else rim + edge
    local_ref[...] = local
    rim_ref[...] = rim


def finish_kernel(g_ref, local_ref, rim_ref, pay_ref, spread_ref, short_ref, out_ref):
    rows, width = g_ref.shape
    low = low_lanes()
    parts = []
    for t in range(width // 128):
        both = pay_ref[t * 16 : t * 16 + 16, :].astype(F32)
        parts.append(jnp.concatenate(unpack((both[:8], both[8:]), low), axis=0))
    nodes = jnp.concatenate(parts, axis=1).astype(BF)
    outside = jnp.dot(spread_ref[...], jnp.concatenate([nodes, nodes], axis=0), preferred_element_type=F32)
    carried = (local_ref[...] + outside[:rows]).astype(BF).astype(F32)
    rim = (rim_ref[...] + outside[rows:]).astype(BF).astype(F32)
    extended = jnp.concatenate([carried, rim], axis=0)
    total = g_ref[...].astype(F32)
    tail = None
    for j in range(SHORT):
        term = short_ref[0, j : j + 1, :] * extended[j : j + rows]
        tail = term if tail is None else tail + term
    out_ref[...] = (total + tail).astype(BF)


PARAMS = pltpu.CompilerParams(vmem_limit_bytes=40 * 1024 * 1024)


def whole(array):
    return pl.BlockSpec(array.shape, lambda i: (0,) * array.ndim)


def on_device(cotangent, gates, short_weight, decay_rates, residues):
    gradient = cotangent[0]
    gates = gates[0]
    short_weight = short_weight[0]
    rates = jnp.swapaxes(decay_rates[0], 1, 2)
    weights = jnp.swapaxes(residues[0], 1, 2)
    rows, channels = gradient.shape
    shards = lax.axis_size("seq")
    segments = lax.axis_size("segment")
    own = channels // shards
    const = constants(rows)
    moment = jnp.asarray(const["moment"])
    spread = jnp.asarray(const["spread"])
    inside = jnp.asarray(const["inside"])
    beyond = jnp.asarray(const["beyond"])
    target_gap = jnp.asarray(const["target_gap"])
    lag_nodes = jnp.asarray(const["lag_nodes"])
    steps = channels // TILE
    owners = TILE // own
    for layer in range(STEPS):
        row_spec = pl.BlockSpec((rows, TILE), lambda i: (0, i))
        gate_spec = pl.BlockSpec((1, rows, TILE), lambda i, layer=layer: (layer, 0, i))
        mode_spec = pl.BlockSpec((1, 16, own), lambda i, layer=layer: (layer, 0, 0))
        pay_spec = pl.BlockSpec((owners * 16, 128), lambda i: (i, 0))
        pay, halo = pl.pallas_call(
            moments_kernel,
            grid=(steps,),
            in_specs=[row_spec, gate_spec, whole(moment), whole(lag_nodes), mode_spec, mode_spec],
            out_specs=[pay_spec, pl.BlockSpec((16, TILE), lambda i: (0, i))],
            out_shape=[
                jax.ShapeDtypeStruct((shards * 16, 128), BF),
                jax.ShapeDtypeStruct((16, channels), BF),
            ],
            scratch_shapes=[pltpu.VMEM((8, 128), F32)],
            compiler_params=PARAMS,
            name="moments",
        )(gradient, gates, moment, lag_nodes, rates, weights)
        halo = lax.ppermute(halo, "seq", [(i, i - 1) for i in range(1, shards)])
        got = lax.all_to_all(pay.reshape(shards, 16, 128), "seq", split_axis=0, concat_axis=0, tiled=True)
        got = got.reshape(shards * 16, 128)
        back = pl.pallas_call(
            lambda *refs: scan_kernel(const["source"], rows, shards, *refs),
            grid=(1,),
            in_specs=[whole(got), mode_spec, mode_spec, whole(target_gap)],
            out_specs=pl.BlockSpec((shards * 8, 128), lambda i: (0, 0)),
            out_shape=jax.ShapeDtypeStruct((shards * 8, 128), BF),
            compiler_params=PARAMS,
            name="scan",
        )(got, rates, weights, target_gap)
        local, rim = pl.pallas_call(
            inside_kernel,
            grid=(steps,),
            in_specs=[row_spec, gate_spec, pl.BlockSpec((16, TILE), lambda i: (0, i)), pay_spec, whole(inside), whole(beyond)],
            out_specs=[row_spec, pl.BlockSpec((8, TILE), lambda i: (0, i))],
            out_shape=[jax.ShapeDtypeStruct((rows, channels), F32), jax.ShapeDtypeStruct((8, channels), F32)],
            compiler_params=PARAMS,
            cost_estimate=pl.CostEstimate(
                flops=2 * NODES * rows * 2 * rows * channels, bytes_accessed=6 * 2**20, transcendentals=0
            ),
            name="inside",
        )(gradient, gates, halo, got, inside, beyond)
        nodes = lax.all_to_all(back.reshape(shards, 8, 128), "seq", split_axis=0, concat_axis=0, tiled=True)
        nodes = nodes.reshape(shards * 8, 128)
        updated = pl.pallas_call(
            finish_kernel,
            grid=(steps,),
            in_specs=[
                row_spec,
                row_spec,
                pl.BlockSpec((8, TILE), lambda i: (0, i)),
                pl.BlockSpec((owners * 8, 128), lambda i: (i, 0)),
                whole(spread),
                pl.BlockSpec((1, SHORT, TILE), lambda i, layer=layer: (layer, 0, i)),
            ],
            out_specs=row_spec,
            out_shape=jax.ShapeDtypeStruct((rows, channels), BF),
            compiler_params=PARAMS,
            name="finish",
        )(gradient, local, rim, nodes, spread, short_weight)
        gradient = lax.ppermute(updated, "segment", [(i, (i - 1) % segments) for i in range(segments)])
    return gradient[None]


def solution(mesh):
    in_specs = (
        P("segment", "seq", None),
        P("segment", None, "seq", None),
        P("segment", None, None, None),
        P("segment", None, "seq", None),
        P("segment", None, "seq", None),
    )
    return jax.shard_map(
        on_device, mesh=mesh, in_specs=in_specs, out_specs=P("segment", "seq", None), check_vma=False
    )
```

```python
import jax
import jax.numpy as jnp
import numpy as np
from jax import lax
from jax.experimental import pallas as pl
from jax.experimental.pallas import tpu as pltpu
from jax.sharding import PartitionSpec as P

MODES = 16
SHORT = 7
NODES = 8
HALF = NODES // 2
RATE_LOW, RATE_HIGH = 3.66e-5, 0.0333334
TILE = 512
VMEM_MIB = 44
BF = jnp.bfloat16
F32 = jnp.float32


def cheb(low, high):
    k = np.arange(NODES)
    x = np.cos(np.pi * (2 * k + 1) / (2 * NODES))
    return 0.5 * (low + high) + 0.5 * (high - low) * x


def cardinal(nodes, points):
    rates = cheb(RATE_LOW, RATE_HIGH)
    points = np.asarray(points, np.float64)
    left = np.exp(-np.outer(rates, nodes)).astype(np.longdouble)
    right = np.exp(-np.outer(rates, points.ravel())).astype(np.longdouble)
    for i in range(len(nodes)):
        pivot = i + int(np.argmax(np.abs(left[i:, i])))
        left[[i, pivot]], right[[i, pivot]] = left[[pivot, i]], right[[pivot, i]]
        right[i] /= left[i, i]
        left[i] /= left[i, i]
        for k in range(len(nodes)):
            if k != i:
                right[k] -= left[k, i] * right[i]
                left[k] -= left[k, i] * left[i]
    return right.astype(np.float64).reshape((len(nodes),) + points.shape)


def split_pair(matrix):
    high = matrix.astype(jnp.bfloat16)
    low = (matrix - high.astype(np.float64)).astype(jnp.bfloat16)
    return np.concatenate([high, low], axis=1)


def constants(rows):
    source = cheb(0.0, rows - 1.0)
    target = cheb(0.0, rows + SHORT - 2.0)
    lags = cheb(2.0 - SHORT, rows - 1.0)
    moment = np.zeros((16, rows))
    basis = cardinal(source, np.arange(rows))
    moment[:HALF] = basis[:HALF]
    moment[8 : 8 + HALF] = basis[HALF:]
    spread = np.zeros((rows + 8, 16))
    basis = cardinal(target, np.arange(rows + SHORT - 1)).T
    for part in range(0, 8, HALF):
        spread[: rows + SHORT - 1, part : part + HALF] = basis[:, :HALF]
        spread[: rows + SHORT - 1, 8 + part : 8 + part + HALF] = basis[:, HALF:]
    place = np.arange(rows)
    lag = place[None, :] - place[:, None]
    inside = cardinal(lags, lag) * (lag >= 0)[None]
    place = np.arange(16)
    lag = place[None, :] - place[:8, None]
    live = (lag < 0) & (place[:8, None] < SHORT - 1)
    beyond = -cardinal(lags, np.where(live, lag, 0)) * live[None]
    wide = np.zeros((NODES * 8 + 16 + rows + 8, 2 * rows), jnp.bfloat16)
    wide[: NODES * 8, :32] = split_pair(beyond.reshape(NODES * 8, 16))
    wide[NODES * 8 : NODES * 8 + 16] = split_pair(moment)
    wide[NODES * 8 + 16 :, :32] = split_pair(spread)
    matrices = np.concatenate([split_pair(inside.reshape(NODES * rows, rows)), wide], axis=0)
    return source, rows - target, lags, matrices


def doubled(x):
    return jnp.concatenate([x, x], axis=1)


def low_lanes():
    return lax.broadcasted_iota(jnp.int32, (8, 128), 1) < 64


def top_rows():
    return lax.broadcasted_iota(jnp.int32, (8, 128), 0) < HALF


def packed_rows(values):
    row = lax.broadcasted_iota(jnp.int32, (8, 128), 0) % HALF
    low = low_lanes()
    out = jnp.zeros((8, 128), F32)
    for r in range(HALF):
        out = jnp.where(row == r, jnp.where(low, F32(values[r]), F32(values[r + HALF])), out)
    return out


def unpack(first, second, low):
    return (
        jnp.where(low, first, pltpu.roll(second, 64, 1)),
        jnp.where(low, pltpu.roll(first, 64, 1), second),
    )


def filter_nodes(rate, res, lags):
    rate, res = doubled(rate), doubled(res)
    place = packed_rows(lags)
    total = jnp.zeros((8, 128), F32)
    for m in range(MODES):
        total = total + res[m : m + 1] * jnp.exp(-rate[m : m + 1] * place)
    return total


def twice(x):
    return jnp.concatenate([x, x], axis=0)


class Rows:
    def __init__(self, rows):
        self.inside = slice(0, NODES * rows)
        self.beyond = slice(NODES * rows, NODES * rows + NODES * 8)
        self.moment = slice(self.beyond.stop, self.beyond.stop + 16)
        self.spread = slice(self.moment.stop, self.moment.stop + rows + 8)


def send_moments(product, matrix, fill, at, pay_ref):
    low, top = low_lanes(), top_rows()
    moments = jnp.dot(matrix, twice(product), preferred_element_type=F32)
    for t in range(product.shape[1] // 128):
        columns = slice(t * 128, t * 128 + 128)
        first, second = unpack(moments[0:8, columns], moments[8:16, columns], low)
        block = jnp.concatenate([jnp.where(top, first, fill), jnp.where(top, second, fill)], axis=0)
        pay_ref[at // 8 + t * 16 : at // 8 + t * 16 + 16, :] = block.astype(BF)


def tiles(channels):
    return [(at, slice(at, at + TILE)) for at in range(0, channels, TILE)]


def first_kernel(lags, g_ref, gate_ref, rate_ref, res_ref, matrix_ref, pay_ref, halo_ref, next_ref):
    where = Rows(g_ref.shape[0])
    next_ref[...] = jnp.concatenate([rate_ref[1], res_ref[1]], axis=0)
    taps = filter_nodes(rate_ref[0], res_ref[0], lags)
    matrix = matrix_ref[where.moment, :]
    for at, cut in tiles(g_ref.shape[1]):
        product = (gate_ref[0, :, cut].astype(F32) * g_ref[:, cut].astype(F32)).astype(BF)
        halo_ref[:, cut] = product[:16]
        send_moments(product, matrix, taps, at, pay_ref)


def scan_body(source, gaps, rows, rate, res, pay_ref, out_ref):
    low, top = low_lanes(), top_rows()
    pairs = pay_ref.shape[0] // 16
    rate, res = doubled(rate), doubled(res)
    enter = []
    for r in range(HALF):
        place = jnp.where(low, F32(source[r]), F32(source[r + HALF]))
        enter.append([jnp.exp(-rate[8 * o : 8 * o + 8] * place) for o in range(2)])
    step = [jnp.exp(-rate[8 * o : 8 * o + 8] * F32(rows)) for o in range(2)]
    gap = packed_rows(gaps)
    leave = [res[m : m + 1] * jnp.exp(-rate[m : m + 1] * gap) for m in range(MODES)]

    def one(block, state):
        total = jnp.zeros((8, 128), F32)
        for m in range(MODES):
            total = total + leave[m] * state[m // 8][m % 8 : m % 8 + 1]
        high = total.astype(BF).astype(F32)
        total = jnp.where(top, high, total - high)
        sums = [None, None]
        for o in range(2):
            part = enter[0][o] * block[0:1]
            for r in range(1, HALF):
                part = part + enter[r][o] * block[r : r + 1]
            sums[o] = part + pltpu.roll(part, 64, 1)
        return total, tuple(step[o] * state[o] + sums[o] for o in range(2))

    def pair(i, state):
        place = pl.ds(pl.multiple_of((pairs - 1 - i) * 16, 16), 16)
        blocks = pay_ref[place, :].astype(F32)
        later, state = one(blocks[8:], state)
        earlier, state = one(blocks[:8], state)
        out_ref[place, :] = jnp.concatenate([earlier, later], axis=0).astype(BF)
        return state

    zero = jnp.zeros((8, 128), F32)
    lax.fori_loop(0, pairs, pair, (zero, zero), unroll=4)


def scan_first_kernel(source, gaps, lags, rows, pay_ref, rate_ref, res_ref, next_ref, out_ref, taps_ref):
    scan_body(source, gaps, rows, rate_ref[0], res_ref[0], pay_ref, out_ref)
    taps_ref[...] = filter_nodes(next_ref[:MODES], next_ref[MODES:], lags)


def scan_last_kernel(source, gaps, rows, pay_ref, next_ref, out_ref):
    scan_body(source, gaps, rows, next_ref[:MODES], next_ref[MODES:], pay_ref, out_ref)


def inside_kernel(g_ref, gate_ref, halo_ref, pay_ref, matrix_ref, local_ref, rim_ref):
    rows, channels = g_ref.shape
    where = Rows(rows)
    low = low_lanes()
    for at, cut in tiles(channels):
        product = (gate_ref[0, :, cut].astype(F32) * g_ref[:, cut].astype(F32)).astype(BF)
        parts = []
        for t in range(at // 128, (at + TILE) // 128):
            both = pay_ref[t * 16 : t * 16 + 16, :].astype(F32)
            parts.append(unpack(both[:8], both[8:], low))
        taps = [jnp.concatenate([part[h] for part in parts], axis=1) for h in range(2)]
        waves = jnp.dot(matrix_ref[where.inside, :], twice(product), preferred_element_type=F32)
        edges = jnp.dot(matrix_ref[where.beyond, :32], twice(halo_ref[:, cut]), preferred_element_type=F32)
        local = None
        rim = None
        for n in range(NODES):
            tap = taps[n // HALF][HALF + n % HALF : HALF + n % HALF + 1]
            wave = tap * waves[n * rows : (n + 1) * rows]
            edge = tap * edges[n * 8 : (n + 1) * 8]
            local = wave if local is None else local + wave
            rim = edge if rim is None else rim + edge
        local_ref[:, cut] = local
        rim_ref[:, cut] = rim


def updated_tile(at, cut, g_ref, local_ref, rim_ref, pay_ref, matrix, short):
    rows = g_ref.shape[0]
    low = low_lanes()
    parts = []
    for t in range(at // 128, (at + TILE) // 128):
        both = pay_ref[t * 16 : t * 16 + 16, :].astype(F32)
        parts.append(jnp.concatenate(unpack(both[:8], both[8:], low), axis=0))
    nodes = jnp.concatenate(parts, axis=1).astype(BF)
    outside = jnp.dot(matrix, twice(nodes), preferred_element_type=F32)
    carried = (local_ref[:, cut] + outside[:rows]).astype(BF).astype(F32)
    rim = (rim_ref[:, cut] + outside[rows:]).astype(BF).astype(F32)
    extended = jnp.concatenate([carried, rim], axis=0)
    tail = None
    for j in range(SHORT):
        term = short[j : j + 1] * extended[j : j + rows]
        tail = term if tail is None else tail + term
    return (g_ref[:, cut].astype(F32) + tail).astype(BF)


def turn_kernel(g_ref, local_ref, rim_ref, nodes_ref, short_ref, gate_ref, matrix_ref, new_ref, pay_ref, halo_ref):
    where = Rows(g_ref.shape[0])
    spread = matrix_ref[where.spread, :32]
    moment = matrix_ref[where.moment, :]
    none = jnp.zeros((8, 128), F32)
    for at, cut in tiles(g_ref.shape[1]):
        new = updated_tile(at, cut, g_ref, local_ref, rim_ref, nodes_ref, spread, short_ref[0, :, cut])
        new_ref[:, cut] = new
        product = (gate_ref[0, :, cut].astype(F32) * new.astype(F32)).astype(BF)
        halo_ref[:, cut] = product[:16]
        send_moments(product, moment, none, at, pay_ref)


def merge_kernel(pay_ref, taps_ref, g_ref, out_ref, same_ref):
    top = top_rows()
    taps = taps_ref[...]
    for t in range(0, pay_ref.shape[0], 16):
        both = pay_ref[t : t + 16, :].astype(F32)
        block = jnp.concatenate([jnp.where(top, both[:8], taps), jnp.where(top, both[8:], taps)], axis=0)
        out_ref[t : t + 16, :] = block.astype(BF)


def last_kernel(g_ref, local_ref, rim_ref, nodes_ref, short_ref, matrix_ref, out_ref):
    spread = matrix_ref[Rows(g_ref.shape[0]).spread, :32]
    for at, cut in tiles(g_ref.shape[1]):
        out_ref[:, cut] = updated_tile(at, cut, g_ref, local_ref, rim_ref, nodes_ref, spread, short_ref[0, :, cut])


PARAMS = pltpu.CompilerParams(vmem_limit_bytes=VMEM_MIB * 1024 * 1024)


def call(kernel, name, ins, outs, fixed=(), layer=0, specs=None, out_specs=None, aliases=None, flops=0):
    def whole(array):
        return pl.BlockSpec(array.shape, lambda i: (0,) * len(array.shape))

    return pl.pallas_call(
        lambda *refs: kernel(*fixed, *refs),
        grid=(1,),
        in_specs=[(specs or {}).get(k) or whole(x) for k, x in enumerate(ins)],
        out_specs=[(out_specs or {}).get(k) or whole(x) for k, x in enumerate(outs)],
        out_shape=list(outs),
        input_output_aliases=aliases or {},
        compiler_params=PARAMS,
        cost_estimate=pl.CostEstimate(flops=flops, bytes_accessed=8 * 2**20, transcendentals=0),
        name=name,
    )(*ins)


def on_device(cotangent, gates, short_weight, decay_rates, residues):
    g = cotangent[0]
    gates = gates[0]
    short_weight = short_weight[0]
    rates = jnp.swapaxes(decay_rates[0], 1, 2)
    weights = jnp.swapaxes(residues[0], 1, 2)
    rows, channels = g.shape
    shards = lax.axis_size("seq")
    segments = lax.axis_size("segment")
    source, gaps, lags, matrices = constants(rows)
    matrices = jnp.asarray(matrices)

    def shape(size, dtype):
        return jax.ShapeDtypeStruct(size, dtype)

    def around(x, distance):
        return lax.ppermute(x, "segment", [(i, (i + distance) % segments) for i in range(segments)])

    def across(x):
        x = x.reshape(shards, 8, 128)
        return lax.all_to_all(x, "seq", split_axis=0, concat_axis=0, tiled=True).reshape(shards * 8, 128)

    pay_shape = shape((shards * 8, 128), BF)
    halo_shape = shape((16, channels), BF)
    row_shape = shape((rows, channels), BF)
    local_shapes = [shape((rows, channels), F32), shape((8, channels), F32)]
    layer_gate = pl.BlockSpec((1, rows, channels), lambda i: (0, 0, 0))
    layer_short = pl.BlockSpec((1, SHORT, channels), lambda i: (0, 0, 0))

    pay, halo, params = call(
        first_kernel, "first", [g, gates, rates, weights, matrices],
        [pay_shape, halo_shape, shape((2 * MODES, channels // shards), F32)],
        fixed=(lags,), specs={1: layer_gate},
    )
    late_gates = gates[1:]
    gates_early = around(late_gates, 1)
    gates_late = around(late_gates, -1)
    params_late = around(params, -1)
    short_late = around(short_weight[1:], -1)
    halo = lax.ppermute(halo, "seq", [(i, i - 1) for i in range(1, shards)])
    got = across(pay)
    back, taps = call(
        scan_first_kernel, "scan", [got, rates, weights, params_late],
        [pay_shape, shape((8, 128), F32)], fixed=(source, gaps, lags, rows),
    )
    nodes = across(back)
    local, rim = call(
        inside_kernel, "inside", [g, gates, halo, got, matrices], local_shapes, specs={1: layer_gate},
        flops=2 * NODES * rows * 2 * rows * channels,
    )
    g, pay, halo = call(
        turn_kernel, "turn", [g, local, rim, nodes, short_weight, gates_early, matrices],
        [row_shape, pay_shape, halo_shape], specs={4: layer_short},
    )
    pay = around(pay, -2)
    moves = [
        (s * shards + k, (s - 2) % segments * shards + k - 1) for s in range(segments) for k in range(1, shards)
    ]
    halo = lax.ppermute(halo, ("segment", "seq"), moves)
    anywhere = pl.BlockSpec(memory_space=pl.ANY)
    pay, g = call(
        merge_kernel, "merge", [pay, taps, g], [pay_shape, row_shape],
        specs={2: anywhere}, out_specs={1: anywhere}, aliases={2: 1},
    )
    g = around(g, -2)
    got = across(pay)
    (back,) = call(
        scan_last_kernel, "scan", [got, params_late], [pay_shape], fixed=(source, gaps, rows)
    )
    nodes = across(back)
    local, rim = call(
        inside_kernel, "inside", [g, gates_late, halo, got, matrices], local_shapes,
        flops=2 * NODES * rows * 2 * rows * channels,
    )
    (g,) = call(last_kernel, "last", [g, local, rim, nodes, short_late, matrices], [row_shape])
    return g[None]


def solution(mesh):
    in_specs = (
        P("segment", "seq", None),
        P("segment", None, "seq", None),
        P("segment", None, None, None),
        P("segment", None, "seq", None),
        P("segment", None, "seq", None),
    )
    return jax.shard_map(
        on_device, mesh=mesh, in_specs=in_specs, out_specs=P("segment", "seq", None), check_vma=False
    )
```

```python
import jax
import jax.numpy as jnp
import numpy as np
from jax import lax
from jax.experimental import pallas as pl
from jax.experimental.pallas import tpu as pltpu
from jax.sharding import PartitionSpec as P

MODES = 16
SHORT = 7
NODES = 8
HALF = NODES // 2
RATE_LOW, RATE_HIGH = 3.66e-5, 0.0333334
TILE = 512
VMEM_MIB = 44
BF = jnp.bfloat16
F32 = jnp.float32


def cheb(low, high):
    k = np.arange(NODES)
    x = np.cos(np.pi * (2 * k + 1) / (2 * NODES))
    return 0.5 * (low + high) + 0.5 * (high - low) * x


def cardinal(nodes, points):
    rates = cheb(RATE_LOW, RATE_HIGH)
    points = np.asarray(points, np.float64)
    left = np.exp(-np.outer(rates, nodes)).astype(np.longdouble)
    right = np.exp(-np.outer(rates, points.ravel())).astype(np.longdouble)
    for i in range(len(nodes)):
        pivot = i + int(np.argmax(np.abs(left[i:, i])))
        left[[i, pivot]], right[[i, pivot]] = left[[pivot, i]], right[[pivot, i]]
        right[i] /= left[i, i]
        left[i] /= left[i, i]
        for k in range(len(nodes)):
            if k != i:
                right[k] -= left[k, i] * right[i]
                left[k] -= left[k, i] * left[i]
    return right.astype(np.float64).reshape((len(nodes),) + points.shape)


def split_pair(matrix):
    high = matrix.astype(jnp.bfloat16)
    low = (matrix - high.astype(np.float64)).astype(jnp.bfloat16)
    return np.concatenate([high, low], axis=1)


def constants(rows):
    source = cheb(0.0, rows - 1.0)
    target = cheb(0.0, rows + SHORT - 2.0)
    lags = cheb(2.0 - SHORT, rows - 1.0)
    moment = np.zeros((16, rows))
    basis = cardinal(source, np.arange(rows))
    moment[:HALF] = basis[:HALF]
    moment[8 : 8 + HALF] = basis[HALF:]
    spread = np.zeros((rows + 8, NODES))
    spread[: rows + SHORT - 1] = cardinal(target, np.arange(rows + SHORT - 1)).T
    place = np.arange(rows)
    lag = place[None, :] - place[:, None]
    inside = cardinal(lags, lag) * (lag >= 0)[None]
    place = np.arange(16)
    lag = place[None, :] - place[:8, None]
    live = (lag < 0) & (place[:8, None] < SHORT - 1)
    beyond = -cardinal(lags, np.where(live, lag, 0)) * live[None]
    wide = np.zeros((NODES * 8 + 16 + rows + 8, 2 * rows), jnp.bfloat16)
    wide[: NODES * 8, :32] = split_pair(beyond.reshape(NODES * 8, 16))
    wide[NODES * 8 : NODES * 8 + 16] = split_pair(moment)
    wide[NODES * 8 + 16 :, : 2 * NODES] = split_pair(spread)
    matrices = np.concatenate([split_pair(inside.reshape(NODES * rows, rows)), wide], axis=0)
    return source, rows - target, lags, matrices


def doubled(x):
    return jnp.concatenate([x, x], axis=1)


def low_lanes():
    return lax.broadcasted_iota(jnp.int32, (8, 128), 1) < 64


def top_rows():
    return lax.broadcasted_iota(jnp.int32, (8, 128), 0) < HALF


def packed_rows(values):
    row = lax.broadcasted_iota(jnp.int32, (8, 128), 0) % HALF
    low = low_lanes()
    out = jnp.zeros((8, 128), F32)
    for r in range(HALF):
        out = jnp.where(row == r, jnp.where(low, F32(values[r]), F32(values[r + HALF])), out)
    return out


def unpack(first, second, low):
    return (
        jnp.where(low, first, pltpu.roll(second, 64, 1)),
        jnp.where(low, pltpu.roll(first, 64, 1), second),
    )


def filter_nodes(rate, res, lags):
    rate, res = doubled(rate), doubled(res)
    place = packed_rows(lags)
    total = jnp.zeros((8, 128), F32)
    for m in range(MODES):
        total = total + res[m : m + 1] * jnp.exp(-rate[m : m + 1] * place)
    return total


def twice(x):
    return jnp.concatenate([x, x], axis=0)


class Rows:
    def __init__(self, rows):
        self.inside = slice(0, NODES * rows)
        self.beyond = slice(NODES * rows, NODES * rows + NODES * 8)
        self.moment = slice(self.beyond.stop, self.beyond.stop + 16)
        self.spread = slice(self.moment.stop, self.moment.stop + rows + 8)


def send_moments(product, matrix, taps, at, pay_ref):
    low, top = low_lanes(), top_rows()
    moments = jnp.dot(matrix, twice(product), preferred_element_type=F32)
    blocks = []
    for t in range(product.shape[1] // 128):
        columns = slice(t * 128, t * 128 + 128)
        first, second = unpack(moments[0:8, columns], moments[8:16, columns], low)
        if taps is None:
            blocks.append(jnp.where(top, first, pltpu.roll(second, HALF, 0)))
        else:
            blocks += [jnp.where(top, first, taps), jnp.where(top, second, taps)]
    for k in range(0, len(blocks), 2):
        start = at // 64 * 8 // (2 if taps is None else 1) + k * 8
        pay_ref[start : start + 16, :] = jnp.concatenate(blocks[k : k + 2], axis=0).astype(BF)


def tiles(channels):
    return [(at, slice(at, at + TILE)) for at in range(0, channels, TILE)]


def first_kernel(lags, g_ref, gate_ref, rate_ref, res_ref, moment_ref, pay_ref, halo_ref, next_ref, late_ref):
    next_ref[...] = jnp.concatenate([rate_ref[1], res_ref[1]], axis=0)
    taps = filter_nodes(rate_ref[0], res_ref[0], lags)
    matrix = moment_ref[...]
    for at, cut in tiles(g_ref.shape[1]):
        product = (gate_ref[0, :, cut].astype(F32) * g_ref[:, cut].astype(F32)).astype(BF)
        halo_ref[:, cut] = product[:16]
        late_ref[:, cut] = gate_ref[1, :, cut]
        send_moments(product, matrix, taps, at, pay_ref)


def scan_body(source, gaps, rows, rate, res, pay_ref, out_ref, taps):
    low, top = low_lanes(), top_rows()
    width = HALF if taps is None else 2 * HALF
    groups = pay_ref.shape[0] // 16
    rate, res = doubled(rate), doubled(res)
    enter = []
    for r in range(HALF):
        place = jnp.where(low, F32(source[r]), F32(source[r + HALF]))
        enter.append([jnp.exp(-rate[8 * o : 8 * o + 8] * place) for o in range(2)])
    step = [jnp.exp(-rate[8 * o : 8 * o + 8] * F32(rows)) for o in range(2)]
    gap = packed_rows(gaps)
    leave = [res[m : m + 1] * jnp.exp(-rate[m : m + 1] * gap) for m in range(MODES)]

    def one(block, state):
        total = jnp.zeros((8, 128), F32)
        for m in range(MODES):
            total = total + leave[m] * state[m // 8][m % 8 : m % 8 + 1]
        sums = [None, None]
        for o in range(2):
            part = enter[0][o] * block[0:1]
            for r in range(1, HALF):
                part = part + enter[r][o] * block[r : r + 1]
            sums[o] = part + pltpu.roll(part, 64, 1)
        return total, tuple(step[o] * state[o] + sums[o] for o in range(2))

    def several(i, state):
        place = pl.ds(pl.multiple_of((groups - 1 - i) * 16, 16), 16)
        blocks = pay_ref[place, :].astype(F32)
        outs = [None] * (16 // width)
        for k in reversed(range(len(outs))):
            outs[k], state = one(blocks[k * width : k * width + HALF], state)
        if taps is None:
            outs = [jnp.where(top, outs[k], outs[k + 1]) for k in range(0, len(outs), 2)]
        else:
            outs = [jnp.where(top, out, taps) for out in outs]
        out_ref[place, :] = jnp.concatenate(outs, axis=0).astype(BF)
        return state

    zero = jnp.zeros((8, 128), F32)
    lax.fori_loop(0, groups, several, (zero, zero), unroll=4 if width == 8 else 2)


def scan_first_kernel(source, gaps, lags, rows, pay_ref, rate_ref, res_ref, next_ref, out_ref):
    taps = filter_nodes(next_ref[:MODES], next_ref[MODES:], lags)
    scan_body(source, gaps, rows, rate_ref[0], res_ref[0], pay_ref, out_ref, taps)


def scan_last_kernel(source, gaps, rows, pay_ref, next_ref, out_ref):
    scan_body(source, gaps, rows, next_ref[:MODES], next_ref[MODES:], pay_ref, out_ref, None)


def inside_kernel(g_ref, gate_ref, halo_ref, pay_ref, matrix_ref, local_ref, rim_ref):
    rows, channels = g_ref.shape
    where = Rows(rows)
    low = low_lanes()
    for at, cut in tiles(channels):
        gate = gate_ref[0, :, cut] if len(gate_ref.shape) == 3 else gate_ref[:, cut]
        product = (gate.astype(F32) * g_ref[:, cut].astype(F32)).astype(BF)
        parts = []
        for t in range(at // 128, (at + TILE) // 128):
            both = pay_ref[t * 16 : t * 16 + 16, :].astype(F32)
            parts.append(unpack(both[:8], both[8:], low))
        taps = [jnp.concatenate([part[h] for part in parts], axis=1) for h in range(2)]
        waves = jnp.dot(matrix_ref[where.inside, :], twice(product), preferred_element_type=F32)
        edges = jnp.dot(matrix_ref[where.beyond, :32], twice(halo_ref[:, cut]), preferred_element_type=F32)
        local = None
        rim = None
        for n in range(NODES):
            tap = taps[n // HALF][HALF + n % HALF : HALF + n % HALF + 1]
            wave = tap * waves[n * rows : (n + 1) * rows]
            edge = tap * edges[n * 8 : (n + 1) * 8]
            local = wave if local is None else local + wave
            rim = edge if rim is None else rim + edge
        local_ref[:, cut] = local
        rim_ref[:, cut] = rim


def updated_tile(at, cut, g_ref, local_ref, rim_ref, pay_ref, matrix, short):
    rows, channels = g_ref.shape
    low, top = low_lanes(), top_rows()
    parts = []
    for t in range(at // 128, (at + TILE) // 128):
        if pay_ref.shape[0] * 8 == channels:
            both = pay_ref[t * 16 : t * 16 + 16, :].astype(F32)
            first, second = unpack(both[:8], both[8:], low)
        else:
            both = pay_ref[t // 2 * 16 : t // 2 * 16 + 16, :].astype(F32)[t % 2 * 8 : t % 2 * 8 + 8]
            first, second = unpack(both, pltpu.roll(both, HALF, 0), low)
        parts.append(jnp.where(top, first, pltpu.roll(second, HALF, 0)))
    nodes = jnp.concatenate(parts, axis=1).astype(BF)
    nodes = jnp.concatenate([nodes, nodes], axis=0)
    outside = jnp.dot(matrix, nodes, preferred_element_type=F32)
    carried = (local_ref[:, cut] + outside[:rows]).astype(BF).astype(F32)
    rim = (rim_ref[:, cut] + outside[rows:]).astype(BF).astype(F32)
    extended = jnp.concatenate([carried, rim], axis=0)
    tail = None
    for j in range(SHORT):
        term = short[j : j + 1] * extended[j : j + rows]
        tail = term if tail is None else tail + term
    return (g_ref[:, cut].astype(F32) + tail).astype(BF)


def turn_kernel(
    g_ref, local_ref, rim_ref, nodes_ref, short_ref, gate_ref, matrix_ref, gate_late, short_late,
    new_ref, pay_ref, halo_ref,
):
    where = Rows(g_ref.shape[0])
    spread = matrix_ref[where.spread, : 2 * NODES]
    moment = matrix_ref[where.moment, :]
    for at, cut in tiles(g_ref.shape[1]):
        new = updated_tile(at, cut, g_ref, local_ref, rim_ref, nodes_ref, spread, short_ref[0, :, cut])
        new_ref[:, cut] = new
        product = (gate_ref[:, cut].astype(F32) * new.astype(F32)).astype(BF)
        halo_ref[:, cut] = product[:16]
        send_moments(product, moment, None, at, pay_ref)


def order_kernel(pay_ref, g_ref, out_ref, same_ref):
    out_ref[...] = pay_ref[...]


def last_kernel(g_ref, local_ref, rim_ref, nodes_ref, short_ref, matrix_ref, out_ref):
    spread = matrix_ref[Rows(g_ref.shape[0]).spread, : 2 * NODES]
    for at, cut in tiles(g_ref.shape[1]):
        out_ref[:, cut] = updated_tile(at, cut, g_ref, local_ref, rim_ref, nodes_ref, spread, short_ref[:, cut])


PARAMS = pltpu.CompilerParams(vmem_limit_bytes=VMEM_MIB * 1024 * 1024)


def call(kernel, name, ins, outs, fixed=(), layer=0, specs=None, out_specs=None, aliases=None, flops=0):
    def whole(array):
        return pl.BlockSpec(array.shape, lambda i: (0,) * len(array.shape))

    return pl.pallas_call(
        lambda *refs: kernel(*fixed, *refs),
        grid=(1,),
        in_specs=[(specs or {}).get(k) or whole(x) for k, x in enumerate(ins)],
        out_specs=[(out_specs or {}).get(k) or whole(x) for k, x in enumerate(outs)],
        out_shape=list(outs),
        input_output_aliases=aliases or {},
        compiler_params=PARAMS,
        cost_estimate=pl.CostEstimate(flops=flops, bytes_accessed=8 * 2**20, transcendentals=0),
        name=name,
    )(*ins)


def in_hbm(x):
    return pltpu.with_memory_space_constraint(x, pltpu.HBM)


def on_device(cotangent, gates, short_weight, decay_rates, residues):
    g = in_hbm(cotangent[0])
    gates = in_hbm(gates[0])
    short_weight = short_weight[0]
    rates = in_hbm(jnp.swapaxes(decay_rates[0], 1, 2))
    weights = in_hbm(jnp.swapaxes(residues[0], 1, 2))
    rows, channels = g.shape
    shards = lax.axis_size("seq")
    segments = lax.axis_size("segment")
    source, gaps, lags, matrices = constants(rows)
    moment = in_hbm(jnp.asarray(matrices[Rows(rows).moment]))
    matrices = jnp.asarray(matrices)

    def shape(size, dtype):
        return jax.ShapeDtypeStruct(size, dtype)

    def around(x, distance):
        return lax.ppermute(x, "segment", [(i, (i + distance) % segments) for i in range(segments)])

    def across(x):
        blocks = x.reshape(shards, x.shape[0] // shards, 128)
        return lax.all_to_all(blocks, "seq", split_axis=0, concat_axis=0, tiled=True).reshape(x.shape)

    pay_shape = shape((shards * 2 * HALF, 128), BF)
    short_pay_shape = shape((shards * HALF, 128), BF)
    halo_shape = shape((16, channels), BF)
    row_shape = shape((rows, channels), BF)
    local_shapes = [shape((rows, channels), F32), shape((8, channels), F32)]
    layer_gate = pl.BlockSpec((1, rows, channels), lambda i: (0, 0, 0))
    layer_short = pl.BlockSpec((1, SHORT, channels), lambda i: (0, 0, 0))

    pay, halo, params, late_gates = call(
        first_kernel, "first", [g, gates, rates, weights, moment],
        [pay_shape, halo_shape, shape((2 * MODES, channels // shards), F32), row_shape],
        fixed=(lags,),
    )
    gates_early = in_hbm(around(late_gates, 1))
    gates_late = in_hbm(around(late_gates, -1))
    params_late = around(params, -1)
    short_late = around(short_weight[1], -1)
    halo = lax.ppermute(halo, "seq", [(i, i - 1) for i in range(1, shards)])
    got = across(pay)
    (back,) = call(
        scan_first_kernel, "scan", [got, rates, weights, params_late], [pay_shape], fixed=(source, gaps, lags, rows)
    )
    nodes = across(back)
    local, rim = call(
        inside_kernel, "inside", [g, gates, halo, got, matrices], local_shapes, specs={1: layer_gate},
        flops=2 * NODES * rows * 2 * rows * channels,
    )
    taps = nodes
    anywhere = pl.BlockSpec(memory_space=pl.ANY)
    g, pay, halo = call(
        turn_kernel, "turn", [g, local, rim, nodes, short_weight, gates_early, matrices, gates_late, short_late],
        [row_shape, short_pay_shape, halo_shape], specs={4: layer_short, 7: anywhere, 8: anywhere},
    )
    pay = around(pay, -2)
    moves = [
        (s * shards + k, (s - 2) % segments * shards + k - 1) for s in range(segments) for k in range(1, shards)
    ]
    halo = lax.ppermute(halo, ("segment", "seq"), moves)
    pay, g = call(
        order_kernel, "order", [pay, g], [short_pay_shape, row_shape],
        specs={1: anywhere}, out_specs={1: anywhere}, aliases={1: 1},
    )
    g = in_hbm(around(g, -2))
    got = across(pay)
    (back,) = call(
        scan_last_kernel, "scan", [got, params_late], [short_pay_shape], fixed=(source, gaps, rows)
    )
    nodes = across(back)
    local, rim = call(
        inside_kernel, "inside", [g, gates_late, halo, taps, matrices], local_shapes,
        flops=2 * NODES * rows * 2 * rows * channels,
    )
    (g,) = call(last_kernel, "last", [g, local, rim, nodes, short_late, matrices], [row_shape])
    return g[None]


def solution(mesh):
    in_specs = (
        P("segment", "seq", None),
        P("segment", None, "seq", None),
        P("segment", None, None, None),
        P("segment", None, "seq", None),
        P("segment", None, "seq", None),
    )
    return jax.shard_map(
        on_device, mesh=mesh, in_specs=in_specs, out_specs=P("segment", "seq", None), check_vma=False
    )
```

```python
import jax
import jax.numpy as jnp
import numpy as np
from jax import lax
from jax.experimental import pallas as pl
from jax.experimental.pallas import tpu as pltpu
from jax.sharding import PartitionSpec as P

MODES = 16
SHORT = 7
NODES = 8
HALF = NODES // 2
RATE_LOW, RATE_HIGH = 3.66e-5, 0.0333334
TILE = 512
VMEM_MIB = 44
BF = jnp.bfloat16
F32 = jnp.float32


def cheb(low, high):
    k = np.arange(NODES)
    x = np.cos(np.pi * (2 * k + 1) / (2 * NODES))
    return 0.5 * (low + high) + 0.5 * (high - low) * x


def cardinal(nodes, points):
    rates = cheb(RATE_LOW, RATE_HIGH)
    points = np.asarray(points, np.float64)
    left = np.exp(-np.outer(rates, nodes)).astype(np.longdouble)
    right = np.exp(-np.outer(rates, points.ravel())).astype(np.longdouble)
    for i in range(len(nodes)):
        pivot = i + int(np.argmax(np.abs(left[i:, i])))
        left[[i, pivot]], right[[i, pivot]] = left[[pivot, i]], right[[pivot, i]]
        right[i] /= left[i, i]
        left[i] /= left[i, i]
        for k in range(len(nodes)):
            if k != i:
                right[k] -= left[k, i] * right[i]
                left[k] -= left[k, i] * left[i]
    return right.astype(np.float64).reshape((len(nodes),) + points.shape)


def split_pair(matrix):
    high = matrix.astype(jnp.bfloat16)
    low = (matrix - high.astype(np.float64)).astype(jnp.bfloat16)
    return np.concatenate([high, low], axis=1)


def constants(rows):
    source = cheb(0.0, rows - 1.0)
    target = cheb(0.0, rows + SHORT - 2.0)
    lags = cheb(2.0 - SHORT, rows - 1.0)
    moment = np.zeros((16, rows))
    basis = cardinal(source, np.arange(rows))
    moment[:HALF] = basis[:HALF]
    moment[8 : 8 + HALF] = basis[HALF:]
    spread = np.zeros((rows + 8, NODES))
    spread[: rows + SHORT - 1] = cardinal(target, np.arange(rows + SHORT - 1)).T
    place = np.arange(rows)
    lag = place[None, :] - place[:, None]
    inside = cardinal(lags, lag) * (lag >= 0)[None]
    place = np.arange(16)
    lag = place[None, :] - place[:8, None]
    live = (lag < 0) & (place[:8, None] < SHORT - 1)
    beyond = -cardinal(lags, np.where(live, lag, 0)) * live[None]
    wide = np.zeros((NODES * 8 + 16 + rows + 8, 2 * rows), jnp.bfloat16)
    wide[: NODES * 8, :32] = split_pair(beyond.reshape(NODES * 8, 16))
    wide[NODES * 8 : NODES * 8 + 16] = split_pair(moment)
    wide[NODES * 8 + 16 :, : 2 * NODES] = split_pair(spread)
    matrices = np.concatenate([split_pair(inside.reshape(NODES * rows, rows)), wide], axis=0)
    return source, rows - target, lags, matrices


def doubled(x):
    return jnp.concatenate([x, x], axis=1)


def low_lanes():
    return lax.broadcasted_iota(jnp.int32, (8, 128), 1) < 64


def top_rows():
    return lax.broadcasted_iota(jnp.int32, (8, 128), 0) < HALF


def packed_rows(values):
    row = lax.broadcasted_iota(jnp.int32, (8, 128), 0) % HALF
    low = low_lanes()
    out = jnp.zeros((8, 128), F32)
    for r in range(HALF):
        out = jnp.where(row == r, jnp.where(low, F32(values[r]), F32(values[r + HALF])), out)
    return out


def unpack(first, second, low):
    return (
        jnp.where(low, first, pltpu.roll(second, 64, 1)),
        jnp.where(low, pltpu.roll(first, 64, 1), second),
    )


def filter_nodes(rate, res, lags):
    rate, res = doubled(rate), doubled(res)
    place = packed_rows(lags)
    total = jnp.zeros((8, 128), F32)
    for m in range(MODES):
        total = total + res[m : m + 1] * jnp.exp(-rate[m : m + 1] * place)
    return total


def twice(x):
    return jnp.concatenate([x, x], axis=0)


class Rows:
    def __init__(self, rows):
        self.inside = slice(0, NODES * rows)
        self.beyond = slice(NODES * rows, NODES * rows + NODES * 8)
        self.moment = slice(self.beyond.stop, self.beyond.stop + 16)
        self.spread = slice(self.moment.stop, self.moment.stop + rows + 8)


def send_moments(product, matrix, taps, at, pay_ref):
    low, top = low_lanes(), top_rows()
    moments = jnp.dot(matrix, twice(product), preferred_element_type=F32)
    blocks = []
    for t in range(product.shape[1] // 128):
        columns = slice(t * 128, t * 128 + 128)
        first, second = unpack(moments[0:8, columns], moments[8:16, columns], low)
        if taps is None:
            blocks.append(jnp.where(top, first, pltpu.roll(second, HALF, 0)))
        else:
            blocks += [jnp.where(top, first, taps), jnp.where(top, second, taps)]
    for k in range(0, len(blocks), 2):
        start = at // 64 * 8 // (2 if taps is None else 1) + k * 8
        pay_ref[start : start + 16, :] = jnp.concatenate(blocks[k : k + 2], axis=0).astype(BF)


def tiles(channels):
    return [(at, slice(at, at + TILE)) for at in range(0, channels, TILE)]


def first_kernel(lags, g_ref, gate_ref, rate_ref, res_ref, moment_ref, pay_ref, halo_ref, next_ref, late_ref):
    next_ref[...] = jnp.concatenate([rate_ref[1], res_ref[1]], axis=0)
    taps = filter_nodes(rate_ref[0], res_ref[0], lags)
    matrix = moment_ref[...]
    for at, cut in tiles(g_ref.shape[1]):
        product = (gate_ref[0, :, cut].astype(F32) * g_ref[:, cut].astype(F32)).astype(BF)
        halo_ref[:, cut] = product[:16]
        late_ref[:, cut] = gate_ref[1, :, cut]
        send_moments(product, matrix, taps, at, pay_ref)


def scan_body(source, gaps, rows, rate, res, pay_ref, out_ref, taps):
    low, top = low_lanes(), top_rows()
    width = HALF if taps is None else 2 * HALF
    groups = pay_ref.shape[0] // 16
    rate, res = doubled(rate), doubled(res)
    enter = []
    for r in range(HALF):
        place = jnp.where(low, F32(source[r]), F32(source[r + HALF]))
        enter.append([jnp.exp(-rate[8 * o : 8 * o + 8] * place) for o in range(2)])
    step = [jnp.exp(-rate[8 * o : 8 * o + 8] * F32(rows)) for o in range(2)]
    gap = packed_rows(gaps)
    leave = [res[m : m + 1] * jnp.exp(-rate[m : m + 1] * gap) for m in range(MODES)]

    def one(block, state):
        total = jnp.zeros((8, 128), F32)
        for m in range(MODES):
            total = total + leave[m] * state[m // 8][m % 8 : m % 8 + 1]
        sums = [None, None]
        for o in range(2):
            part = enter[0][o] * block[0:1]
            for r in range(1, HALF):
                part = part + enter[r][o] * block[r : r + 1]
            sums[o] = part + pltpu.roll(part, 64, 1)
        return total, tuple(step[o] * state[o] + sums[o] for o in range(2))

    def several(i, state):
        place = pl.ds(pl.multiple_of((groups - 1 - i) * 16, 16), 16)
        blocks = pay_ref[place, :].astype(F32)
        outs = [None] * (16 // width)
        for k in reversed(range(len(outs))):
            outs[k], state = one(blocks[k * width : k * width + HALF], state)
        if taps is None:
            outs = [jnp.where(top, outs[k], outs[k + 1]) for k in range(0, len(outs), 2)]
        else:
            outs = [jnp.where(top, out, taps) for out in outs]
        out_ref[place, :] = jnp.concatenate(outs, axis=0).astype(BF)
        return state

    zero = jnp.zeros((8, 128), F32)
    lax.fori_loop(0, groups, several, (zero, zero), unroll=4 if width == 8 else 2)


def scan_first_kernel(source, gaps, lags, rows, pay_ref, rate_ref, res_ref, next_ref, out_ref):
    taps = filter_nodes(next_ref[:MODES], next_ref[MODES:], lags)
    scan_body(source, gaps, rows, rate_ref[0], res_ref[0], pay_ref, out_ref, taps)


def scan_last_kernel(source, gaps, rows, pay_ref, next_ref, out_ref):
    scan_body(source, gaps, rows, next_ref[:MODES], next_ref[MODES:], pay_ref, out_ref, None)


def inside_kernel(g_ref, gate_ref, halo_ref, pay_ref, matrix_ref, local_ref, rim_ref):
    rows, channels = g_ref.shape
    where = Rows(rows)
    low = low_lanes()
    for at, cut in tiles(channels):
        gate = gate_ref[0, :, cut] if len(gate_ref.shape) == 3 else gate_ref[:, cut]
        product = (gate.astype(F32) * g_ref[:, cut].astype(F32)).astype(BF)
        parts = []
        for t in range(at // 128, (at + TILE) // 128):
            both = pay_ref[t * 16 : t * 16 + 16, :].astype(F32)
            parts.append(unpack(both[:8], both[8:], low))
        taps = [jnp.concatenate([part[h] for part in parts], axis=1) for h in range(2)]
        waves = jnp.dot(matrix_ref[where.inside, :], twice(product), preferred_element_type=F32)
        edges = jnp.dot(matrix_ref[where.beyond, :32], twice(halo_ref[:, cut]), preferred_element_type=F32)
        local = None
        rim = None
        for n in range(NODES):
            tap = taps[n // HALF][HALF + n % HALF : HALF + n % HALF + 1]
            wave = tap * waves[n * rows : (n + 1) * rows]
            edge = tap * edges[n * 8 : (n + 1) * 8]
            local = wave if local is None else local + wave
            rim = edge if rim is None else rim + edge
        local_ref[:, cut] = local
        rim_ref[:, cut] = rim


class Fetch:
    def __init__(self, far, near, sems):
        self.near = near
        self.copies = [
            pltpu.make_async_copy(far.at[:, cut], near.at[:, cut], sems.at[k])
            for k, (_, cut) in enumerate(tiles(near.shape[1]))
        ]

    def start(self, at):
        self.copies[at // TILE].start()

    def tile(self, at):
        self.copies[at // TILE].wait()
        return self.near[:, at : at + TILE].astype(F32)


def updated_tile(at, cut, g, local_ref, rim_ref, pay_ref, matrix, short):
    rows, channels = g.near.shape
    low, top = low_lanes(), top_rows()
    parts = []
    for t in range(at // 128, (at + TILE) // 128):
        if pay_ref.shape[0] * 8 == channels:
            both = pay_ref[t * 16 : t * 16 + 16, :].astype(F32)
            first, second = unpack(both[:8], both[8:], low)
        else:
            both = pay_ref[t // 2 * 16 : t // 2 * 16 + 16, :].astype(F32)[t % 2 * 8 : t % 2 * 8 + 8]
            first, second = unpack(both, pltpu.roll(both, HALF, 0), low)
        parts.append(jnp.where(top, first, pltpu.roll(second, HALF, 0)))
    nodes = jnp.concatenate(parts, axis=1).astype(BF)
    nodes = jnp.concatenate([nodes, nodes], axis=0)
    outside = jnp.dot(matrix, nodes, preferred_element_type=F32)
    carried = (local_ref[:, cut] + outside[:rows]).astype(BF).astype(F32)
    rim = (rim_ref[:, cut] + outside[rows:]).astype(BF).astype(F32)
    extended = jnp.concatenate([carried, rim], axis=0)
    tail = None
    for j in range(SHORT):
        term = short[j : j + 1] * extended[j : j + rows]
        tail = term if tail is None else tail + term
    return (g.tile(at) + tail).astype(BF)


def turn_kernel(
    g_far, local_ref, rim_ref, nodes_ref, short_ref, gate_far, matrix_ref, gate_late, short_late,
    new_far, pay_ref, halo_ref, g_near, gate_near, new_near, g_sem, gate_sem, new_sem,
):
    where = Rows(g_near.shape[0])
    g, gate = Fetch(g_far, g_near, g_sem), Fetch(gate_far, gate_near, gate_sem)
    out = Fetch(new_near, new_far, new_sem)
    for at, _ in tiles(g_near.shape[1]):
        g.start(at)
        gate.start(at)
    spread = matrix_ref[where.spread, : 2 * NODES]
    moment = matrix_ref[where.moment, :]
    for at, cut in tiles(g_near.shape[1]):
        new = updated_tile(at, cut, g, local_ref, rim_ref, nodes_ref, spread, short_ref[0, :, cut])
        new_near[:, cut] = new
        out.start(at)
        product = (gate.tile(at) * new.astype(F32)).astype(BF)
        halo_ref[:, cut] = product[:16]
        send_moments(product, moment, None, at, pay_ref)
    for copy in out.copies:
        copy.wait()


def last_kernel(
    g_far, local_ref, rim_ref, nodes_ref, short_ref, matrix_ref, out_far, g_near, out_near, g_sem, out_sem
):
    spread = matrix_ref[Rows(g_near.shape[0]).spread, : 2 * NODES]
    g, out = Fetch(g_far, g_near, g_sem), Fetch(out_near, out_far, out_sem)
    for at, _ in tiles(g_near.shape[1]):
        g.start(at)
    for at, cut in tiles(g_near.shape[1]):
        out_near[:, cut] = updated_tile(at, cut, g, local_ref, rim_ref, nodes_ref, spread, short_ref[:, cut])
        out.start(at)
    for copy in out.copies:
        copy.wait()


PARAMS = pltpu.CompilerParams(vmem_limit_bytes=VMEM_MIB * 1024 * 1024)


def call(kernel, name, ins, outs, fixed=(), specs=None, out_specs=None, flops=0, scratch=None):
    def whole(array):
        if scratch:
            return pl.BlockSpec(memory_space=pltpu.VMEM)
        return pl.BlockSpec(array.shape, lambda i: (0,) * len(array.shape))

    return pl.pallas_call(
        lambda *refs: kernel(*fixed, *refs),
        **({"scratch_shapes": scratch} if scratch else {"grid": (1,)}),
        in_specs=[(specs or {}).get(k) or whole(x) for k, x in enumerate(ins)],
        out_specs=[(out_specs or {}).get(k) or whole(x) for k, x in enumerate(outs)],
        out_shape=list(outs),
        compiler_params=PARAMS,
        cost_estimate=pl.CostEstimate(flops=flops, bytes_accessed=8 * 2**20, transcendentals=0),
        name=name,
    )(*ins)


def in_hbm(x):
    return pltpu.with_memory_space_constraint(x, pltpu.HBM)


def on_device(cotangent, gates, short_weight, decay_rates, residues):
    g = in_hbm(cotangent[0])
    gates = in_hbm(gates[0])
    short_weight = short_weight[0]
    rates = in_hbm(jnp.swapaxes(decay_rates[0], 1, 2))
    weights = in_hbm(jnp.swapaxes(residues[0], 1, 2))
    rows, channels = g.shape
    shards = lax.axis_size("seq")
    segments = lax.axis_size("segment")
    source, gaps, lags, matrices = constants(rows)
    moment = in_hbm(jnp.asarray(matrices[Rows(rows).moment]))
    matrices = jnp.asarray(matrices)

    def shape(size, dtype):
        return jax.ShapeDtypeStruct(size, dtype)

    def around(x, distance):
        return lax.ppermute(x, "segment", [(i, (i + distance) % segments) for i in range(segments)])

    def across(x):
        blocks = x.reshape(shards, x.shape[0] // shards, 128)
        return lax.all_to_all(blocks, "seq", split_axis=0, concat_axis=0, tiled=True).reshape(x.shape)

    pay_shape = shape((shards * 2 * HALF, 128), BF)
    short_pay_shape = shape((shards * HALF, 128), BF)
    halo_shape = shape((16, channels), BF)
    row_shape = shape((rows, channels), BF)
    local_shapes = [shape((rows, channels), F32), shape((8, channels), F32)]
    layer_gate = pl.BlockSpec((1, rows, channels), lambda i: (0, 0, 0))

    pay, halo, params, late_gates = call(
        first_kernel, "first", [g, gates, rates, weights, moment],
        [pay_shape, halo_shape, shape((2 * MODES, channels // shards), F32), row_shape],
        fixed=(lags,),
    )
    gates_early = in_hbm(around(late_gates, 1))
    gates_late = in_hbm(around(late_gates, -1))
    params_late = around(params, -1)
    params_early = around(params, 1)
    short_late = around(short_weight[1], -1)
    halo = lax.ppermute(halo, "seq", [(i, i - 1) for i in range(1, shards)])
    got = across(pay)
    (back,) = call(
        scan_first_kernel, "scan", [got, rates, weights, params_late], [pay_shape], fixed=(source, gaps, lags, rows)
    )
    nodes = across(back)
    local, rim = call(
        inside_kernel, "inside", [g, gates, halo, got, matrices], local_shapes, specs={1: layer_gate},
        flops=2 * NODES * rows * 2 * rows * channels,
    )
    taps = nodes
    anywhere = pl.BlockSpec(memory_space=pl.ANY)
    near = [pltpu.VMEM((rows, channels), BF)]
    sems = [pltpu.SemaphoreType.DMA((channels // TILE,))]
    g, pay, halo = call(
        turn_kernel, "turn", [g, local, rim, nodes, short_weight, gates_early, matrices, gates_late, short_late],
        [row_shape, short_pay_shape, halo_shape],
        specs={0: anywhere, 5: anywhere, 7: anywhere, 8: anywhere}, out_specs={0: anywhere},
        scratch=near * 3 + sems * 3,
    )
    moves = [
        (s * shards + k, (s - 2) % segments * shards + k - 1) for s in range(segments) for k in range(1, shards)
    ]
    halo = lax.ppermute(halo, ("segment", "seq"), moves)
    g = in_hbm(around(g, -2))
    got = across(pay)
    (back,) = call(
        scan_last_kernel, "scan", [got, params_early], [short_pay_shape], fixed=(source, gaps, rows)
    )
    nodes = around(across(back), -2)
    local, rim = call(
        inside_kernel, "inside", [g, gates_late, halo, taps, matrices], local_shapes,
        flops=2 * NODES * rows * 2 * rows * channels,
    )
    (g,) = call(
        last_kernel, "last", [g, local, rim, nodes, short_late, matrices], [row_shape],
        specs={0: anywhere}, out_specs={0: anywhere}, scratch=near * 2 + sems * 2,
    )
    return g[None]


def solution(mesh):
    in_specs = (
        P("segment", "seq", None),
        P("segment", None, "seq", None),
        P("segment", None, None, None),
        P("segment", None, "seq", None),
        P("segment", None, "seq", None),
    )
    return jax.shard_map(
        on_device, mesh=mesh, in_specs=in_specs, out_specs=P("segment", "seq", None), check_vma=False
    )
```

```python
import jax
import jax.numpy as jnp
import numpy as np
from jax import lax
from jax.experimental import pallas as pl
from jax.experimental.pallas import tpu as pltpu
from jax.sharding import PartitionSpec as P

MODES = 16
SHORT = 7
NODES = 8
HALF = NODES // 2
RATE_LOW, RATE_HIGH = 3.66e-5, 0.0333334
TILE = 512
VMEM_MIB = 44
BF = jnp.bfloat16
F32 = jnp.float32


def cheb(low, high):
    k = np.arange(NODES)
    x = np.cos(np.pi * (2 * k + 1) / (2 * NODES))
    return 0.5 * (low + high) + 0.5 * (high - low) * x


def cardinal(nodes, points):
    rates = cheb(RATE_LOW, RATE_HIGH)
    points = np.asarray(points, np.float64)
    left = np.exp(-np.outer(rates, nodes)).astype(np.longdouble)
    right = np.exp(-np.outer(rates, points.ravel())).astype(np.longdouble)
    for i in range(len(nodes)):
        pivot = i + int(np.argmax(np.abs(left[i:, i])))
        left[[i, pivot]], right[[i, pivot]] = left[[pivot, i]], right[[pivot, i]]
        right[i] /= left[i, i]
        left[i] /= left[i, i]
        for k in range(len(nodes)):
            if k != i:
                right[k] -= left[k, i] * right[i]
                left[k] -= left[k, i] * left[i]
    return right.astype(np.float64).reshape((len(nodes),) + points.shape)


def split_pair(matrix):
    high = matrix.astype(jnp.bfloat16)
    low = (matrix - high.astype(np.float64)).astype(jnp.bfloat16)
    return np.concatenate([high, low], axis=1)


def constants(rows):
    source = cheb(0.0, rows - 1.0)
    target = cheb(0.0, rows + SHORT - 2.0)
    lags = cheb(2.0 - SHORT, rows - 1.0)
    moment = np.zeros((16, rows))
    basis = cardinal(source, np.arange(rows))
    moment[:HALF] = basis[:HALF]
    moment[8 : 8 + HALF] = basis[HALF:]
    spread = np.zeros((rows + 8, NODES))
    spread[: rows + SHORT - 1] = cardinal(target, np.arange(rows + SHORT - 1)).T
    place = np.arange(rows)
    lag = place[None, :] - place[:, None]
    inside = cardinal(lags, lag) * (lag >= 0)[None]
    place = np.arange(16)
    lag = place[None, :] - place[:8, None]
    live = (lag < 0) & (place[:8, None] < SHORT - 1)
    beyond = -cardinal(lags, np.where(live, lag, 0)) * live[None]
    wide = np.zeros((NODES * 8 + 16 + rows + 8, 2 * rows), jnp.bfloat16)
    wide[: NODES * 8, :32] = split_pair(beyond.reshape(NODES * 8, 16))
    wide[NODES * 8 : NODES * 8 + 16] = split_pair(moment)
    wide[NODES * 8 + 16 :, : 2 * NODES] = split_pair(spread)
    matrices = np.concatenate([split_pair(inside.reshape(NODES * rows, rows)), wide], axis=0)
    return source, rows - target, lags, matrices


def doubled(x):
    return jnp.concatenate([x, x], axis=1)


def low_lanes():
    return lax.broadcasted_iota(jnp.int32, (8, 128), 1) < 64


def top_rows():
    return lax.broadcasted_iota(jnp.int32, (8, 128), 0) < HALF


def packed_rows(values):
    row = lax.broadcasted_iota(jnp.int32, (8, 128), 0) % HALF
    low = low_lanes()
    out = jnp.zeros((8, 128), F32)
    for r in range(HALF):
        out = jnp.where(row == r, jnp.where(low, F32(values[r]), F32(values[r + HALF])), out)
    return out


def unpack(first, second, low):
    return (
        jnp.where(low, first, pltpu.roll(second, 64, 1)),
        jnp.where(low, pltpu.roll(first, 64, 1), second),
    )


def filter_nodes(rate, res, lags):
    rate, res = doubled(rate), doubled(res)
    place = packed_rows(lags)
    total = jnp.zeros((8, 128), F32)
    for m in range(MODES):
        total = total + res[m : m + 1] * jnp.exp(-rate[m : m + 1] * place)
    return total


def twice(x):
    return jnp.concatenate([x, x], axis=0)


class Rows:
    def __init__(self, rows):
        self.inside = slice(0, NODES * rows)
        self.beyond = slice(NODES * rows, NODES * rows + NODES * 8)
        self.moment = slice(self.beyond.stop, self.beyond.stop + 16)
        self.spread = slice(self.moment.stop, self.moment.stop + rows + 8)


def send_moments(product, matrix, taps, at, pay_ref):
    low, top = low_lanes(), top_rows()
    moments = jnp.dot(matrix, twice(product), preferred_element_type=F32)
    blocks = []
    for t in range(product.shape[1] // 128):
        columns = slice(t * 128, t * 128 + 128)
        first, second = unpack(moments[0:8, columns], moments[8:16, columns], low)
        if taps is None:
            blocks.append(jnp.where(top, first, pltpu.roll(second, HALF, 0)))
        else:
            blocks += [jnp.where(top, first, taps), jnp.where(top, second, taps)]
    for k in range(0, len(blocks), 2):
        start = at // 64 * 8 // (2 if taps is None else 1) + k * 8
        pay_ref[start : start + 16, :] = jnp.concatenate(blocks[k : k + 2], axis=0).astype(BF)


def tiles(channels):
    return [(at, slice(at, at + TILE)) for at in range(0, channels, TILE)]


def first_kernel(lags, g_ref, gate_ref, rate_ref, res_ref, moment_ref, pay_ref, halo_ref, next_ref, late_ref):
    next_ref[...] = jnp.concatenate([rate_ref[1], res_ref[1]], axis=0)
    taps = filter_nodes(rate_ref[0], res_ref[0], lags)
    matrix = moment_ref[...]
    for at, cut in tiles(g_ref.shape[1]):
        product = (gate_ref[0, :, cut].astype(F32) * g_ref[:, cut].astype(F32)).astype(BF)
        halo_ref[:, cut] = product[:16]
        late_ref[:, cut] = gate_ref[1, :, cut]
        send_moments(product, matrix, taps, at, pay_ref)


def scan_body(source, gaps, rows, rate, res, pay_ref, out_ref, taps):
    low, top = low_lanes(), top_rows()
    width = HALF if taps is None else 2 * HALF
    groups = pay_ref.shape[0] // 16
    rate, res = doubled(rate), doubled(res)
    enter = []
    for r in range(HALF):
        place = jnp.where(low, F32(source[r]), F32(source[r + HALF]))
        enter.append([jnp.exp(-rate[8 * o : 8 * o + 8] * place) for o in range(2)])
    step = [jnp.exp(-rate[8 * o : 8 * o + 8] * F32(rows)) for o in range(2)]
    gap = packed_rows(gaps)
    leave = [res[m : m + 1] * jnp.exp(-rate[m : m + 1] * gap) for m in range(MODES)]

    def one(block, state):
        total = jnp.zeros((8, 128), F32)
        for m in range(MODES):
            total = total + leave[m] * state[m // 8][m % 8 : m % 8 + 1]
        sums = [None, None]
        for o in range(2):
            part = enter[0][o] * block[0:1]
            for r in range(1, HALF):
                part = part + enter[r][o] * block[r : r + 1]
            sums[o] = part + pltpu.roll(part, 64, 1)
        return total, tuple(step[o] * state[o] + sums[o] for o in range(2))

    def several(i, state):
        place = pl.ds(pl.multiple_of((groups - 1 - i) * 16, 16), 16)
        blocks = pay_ref[place, :].astype(F32)
        outs = [None] * (16 // width)
        for k in reversed(range(len(outs))):
            outs[k], state = one(blocks[k * width : k * width + HALF], state)
        if taps is None:
            outs = [jnp.where(top, outs[k], outs[k + 1]) for k in range(0, len(outs), 2)]
        else:
            outs = [jnp.where(top, out, taps) for out in outs]
        out_ref[place, :] = jnp.concatenate(outs, axis=0).astype(BF)
        return state

    zero = jnp.zeros((8, 128), F32)
    lax.fori_loop(0, groups, several, (zero, zero), unroll=4 if width == 8 else 2)


def scan_first_kernel(source, gaps, lags, rows, pay_ref, rate_ref, res_ref, next_ref, out_ref):
    taps = filter_nodes(next_ref[:MODES], next_ref[MODES:], lags)
    scan_body(source, gaps, rows, rate_ref[0], res_ref[0], pay_ref, out_ref, taps)


def scan_last_kernel(source, gaps, rows, pay_ref, next_ref, out_ref):
    scan_body(source, gaps, rows, next_ref[:MODES], next_ref[MODES:], pay_ref, out_ref, None)


def inside_kernel(g_ref, gate_ref, halo_ref, pay_ref, matrix_ref, local_ref, rim_ref):
    rows, channels = g_ref.shape
    where = Rows(rows)
    low = low_lanes()
    for at, cut in tiles(channels):
        gate = gate_ref[0, :, cut] if len(gate_ref.shape) == 3 else gate_ref[:, cut]
        product = (gate.astype(F32) * g_ref[:, cut].astype(F32)).astype(BF)
        parts = []
        for t in range(at // 128, (at + TILE) // 128):
            both = pay_ref[t * 16 : t * 16 + 16, :].astype(F32)
            parts.append(unpack(both[:8], both[8:], low))
        taps = [jnp.concatenate([part[h] for part in parts], axis=1) for h in range(2)]
        waves = jnp.dot(matrix_ref[where.inside, :], twice(product), preferred_element_type=F32)
        edges = jnp.dot(matrix_ref[where.beyond, :32], twice(halo_ref[:, cut]), preferred_element_type=F32)
        local = None
        rim = None
        for n in range(NODES):
            tap = taps[n // HALF][HALF + n % HALF : HALF + n % HALF + 1]
            wave = tap * waves[n * rows : (n + 1) * rows]
            edge = tap * edges[n * 8 : (n + 1) * 8]
            local = wave if local is None else local + wave
            rim = edge if rim is None else rim + edge
        local_ref[:, cut] = local
        rim_ref[:, cut] = rim


class Fetch:
    def __init__(self, far, near, sems):
        self.near = near
        self.copies = [
            pltpu.make_async_copy(far.at[:, cut], near.at[:, cut], sems.at[k])
            for k, (_, cut) in enumerate(tiles(near.shape[1]))
        ]

    def start(self, at):
        self.copies[at // TILE].start()

    def tile(self, at):
        self.copies[at // TILE].wait()
        return self.near[:, at : at + TILE].astype(F32)


def updated_tile(at, cut, g, local_ref, rim_ref, pay_ref, matrix, short):
    rows, channels = g.near.shape
    low, top = low_lanes(), top_rows()
    parts = []
    for t in range(at // 128, (at + TILE) // 128):
        if pay_ref.shape[0] * 8 == channels:
            both = pay_ref[t * 16 : t * 16 + 16, :].astype(F32)
            first, second = unpack(both[:8], both[8:], low)
        else:
            both = pay_ref[t // 2 * 16 : t // 2 * 16 + 16, :].astype(F32)[t % 2 * 8 : t % 2 * 8 + 8]
            first, second = unpack(both, pltpu.roll(both, HALF, 0), low)
        parts.append(jnp.where(top, first, pltpu.roll(second, HALF, 0)))
    nodes = jnp.concatenate(parts, axis=1).astype(BF)
    nodes = jnp.concatenate([nodes, nodes], axis=0)
    outside = jnp.dot(matrix, nodes, preferred_element_type=F32)
    carried = (local_ref[:, cut] + outside[:rows]).astype(BF).astype(F32)
    rim = (rim_ref[:, cut] + outside[rows:]).astype(BF).astype(F32)
    extended = jnp.concatenate([carried, rim], axis=0)
    tail = None
    for j in range(SHORT):
        term = short[j : j + 1] * extended[j : j + rows]
        tail = term if tail is None else tail + term
    return (g.tile(at) + tail).astype(BF)


def turn_kernel(
    g_far, local_ref, rim_ref, nodes_ref, short_ref, gate_far, matrix_ref, gate_late, short_late,
    new_far, pay_ref, halo_ref, g_near, gate_near, new_near, g_sem, gate_sem, new_sem,
):
    where = Rows(g_near.shape[0])
    g, gate = Fetch(g_far, g_near, g_sem), Fetch(gate_far, gate_near, gate_sem)
    out = Fetch(new_near, new_far, new_sem)
    for at, _ in tiles(g_near.shape[1]):
        g.start(at)
        gate.start(at)
    spread = matrix_ref[where.spread, : 2 * NODES]
    moment = matrix_ref[where.moment, :]
    for at, cut in tiles(g_near.shape[1]):
        new = updated_tile(at, cut, g, local_ref, rim_ref, nodes_ref, spread, short_ref[0, :, cut])
        new_near[:, cut] = new
        out.start(at)
        product = (gate.tile(at) * new.astype(F32)).astype(BF)
        halo_ref[:, cut] = product[:16]
        send_moments(product, moment, None, at, pay_ref)
    for copy in out.copies:
        copy.wait()


def order_kernel(nodes_ref, rim_ref, out_ref):
    out_ref[...] = nodes_ref[...]


def last_kernel(
    g_far, local_ref, rim_ref, nodes_ref, short_ref, matrix_ref, out_far, g_near, out_near, g_sem, out_sem
):
    spread = matrix_ref[Rows(g_near.shape[0]).spread, : 2 * NODES]
    g, out = Fetch(g_far, g_near, g_sem), Fetch(out_near, out_far, out_sem)
    for at, _ in tiles(g_near.shape[1]):
        g.start(at)
    for at, cut in tiles(g_near.shape[1]):
        out_near[:, cut] = updated_tile(at, cut, g, local_ref, rim_ref, nodes_ref, spread, short_ref[:, cut])
        out.start(at)
    for copy in out.copies:
        copy.wait()


PARAMS = pltpu.CompilerParams(vmem_limit_bytes=VMEM_MIB * 1024 * 1024)


def call(kernel, name, ins, outs, fixed=(), specs=None, out_specs=None, flops=0, scratch=None):
    def whole(array):
        if scratch:
            return pl.BlockSpec(memory_space=pltpu.VMEM)
        return pl.BlockSpec(array.shape, lambda i: (0,) * len(array.shape))

    return pl.pallas_call(
        lambda *refs: kernel(*fixed, *refs),
        **({"scratch_shapes": scratch} if scratch else {"grid": (1,)}),
        in_specs=[(specs or {}).get(k) or whole(x) for k, x in enumerate(ins)],
        out_specs=[(out_specs or {}).get(k) or whole(x) for k, x in enumerate(outs)],
        out_shape=list(outs),
        compiler_params=PARAMS,
        cost_estimate=pl.CostEstimate(flops=flops, bytes_accessed=8 * 2**20, transcendentals=0),
        name=name,
    )(*ins)


def in_hbm(x):
    return pltpu.with_memory_space_constraint(x, pltpu.HBM)


def on_device(cotangent, gates, short_weight, decay_rates, residues):
    g = in_hbm(cotangent[0])
    gates = in_hbm(gates[0])
    short_weight = short_weight[0]
    rates = in_hbm(jnp.swapaxes(decay_rates[0], 1, 2))
    weights = in_hbm(jnp.swapaxes(residues[0], 1, 2))
    rows, channels = g.shape
    shards = lax.axis_size("seq")
    segments = lax.axis_size("segment")
    source, gaps, lags, matrices = constants(rows)
    moment = in_hbm(jnp.asarray(matrices[Rows(rows).moment]))
    matrices = jnp.asarray(matrices)

    def shape(size, dtype):
        return jax.ShapeDtypeStruct(size, dtype)

    def around(x, distance):
        return lax.ppermute(x, "segment", [(i, (i + distance) % segments) for i in range(segments)])

    def across(x):
        blocks = x.reshape(shards, x.shape[0] // shards, 128)
        return lax.all_to_all(blocks, "seq", split_axis=0, concat_axis=0, tiled=True).reshape(x.shape)

    pay_shape = shape((shards * 2 * HALF, 128), BF)
    short_pay_shape = shape((shards * HALF, 128), BF)
    halo_shape = shape((16, channels), BF)
    row_shape = shape((rows, channels), BF)
    local_shapes = [shape((rows, channels), F32), shape((8, channels), F32)]
    layer_gate = pl.BlockSpec((1, rows, channels), lambda i: (0, 0, 0))

    pay, halo, params, late_gates = call(
        first_kernel, "first", [g, gates, rates, weights, moment],
        [pay_shape, halo_shape, shape((2 * MODES, channels // shards), F32), row_shape],
        fixed=(lags,),
    )
    gates_early = in_hbm(around(late_gates, 1))
    gates_late = in_hbm(around(late_gates, -1))
    params_late = around(params, -1)
    params_early = around(params, 1)
    short_late = around(short_weight[1], -1)
    halo = lax.ppermute(halo, "seq", [(i, i - 1) for i in range(1, shards)])
    got = across(pay)
    (back,) = call(
        scan_first_kernel, "scan", [got, rates, weights, params_late], [pay_shape], fixed=(source, gaps, lags, rows)
    )
    nodes = across(back)
    local, rim = call(
        inside_kernel, "inside", [g, gates, halo, got, matrices], local_shapes, specs={1: layer_gate},
        flops=2 * NODES * rows * 2 * rows * channels,
    )
    taps = nodes
    anywhere = pl.BlockSpec(memory_space=pl.ANY)
    near = [pltpu.VMEM((rows, channels), BF)]
    sems = [pltpu.SemaphoreType.DMA((channels // TILE,))]
    g, pay, halo = call(
        turn_kernel, "turn", [g, local, rim, nodes, short_weight, gates_early, matrices, gates_late, short_late],
        [row_shape, short_pay_shape, halo_shape],
        specs={0: anywhere, 5: anywhere, 7: anywhere, 8: anywhere}, out_specs={0: anywhere},
        scratch=near * 3 + sems * 3,
    )
    moves = [
        (s * shards + k, (s - 2) % segments * shards + k - 1) for s in range(segments) for k in range(1, shards)
    ]
    halo = lax.ppermute(halo, ("segment", "seq"), moves)
    g = in_hbm(around(g, -2))
    got = across(pay)
    (back,) = call(
        scan_last_kernel, "scan", [got, params_early], [short_pay_shape], fixed=(source, gaps, rows)
    )
    nodes = across(back)
    local, rim = call(
        inside_kernel, "inside", [g, gates_late, halo, taps, matrices], local_shapes,
        flops=2 * NODES * rows * 2 * rows * channels,
    )
    nodes = pl.pallas_call(
        order_kernel,
        in_specs=[pl.BlockSpec(memory_space=pltpu.VMEM), anywhere],
        out_specs=pl.BlockSpec(memory_space=pltpu.VMEM),
        out_shape=short_pay_shape,
        compiler_params=PARAMS,
        name="order",
    )(nodes, rim)
    nodes = around(nodes, -2)
    (g,) = call(
        last_kernel, "last", [g, local, rim, nodes, short_late, matrices], [row_shape],
        specs={0: anywhere}, out_specs={0: anywhere}, scratch=near * 2 + sems * 2,
    )
    return g[None]


def solution(mesh):
    in_specs = (
        P("segment", "seq", None),
        P("segment", None, "seq", None),
        P("segment", None, None, None),
        P("segment", None, "seq", None),
        P("segment", None, "seq", None),
    )
    return jax.shard_map(
        on_device, mesh=mesh, in_specs=in_specs, out_specs=P("segment", "seq", None), check_vma=False
    )
```

```python
import jax
import jax.numpy as jnp
import numpy as np
from jax import lax
from jax.experimental import pallas as pl
from jax.experimental.pallas import tpu as pltpu
from jax.sharding import PartitionSpec as P

MODES = 16
SHORT = 7
NODES = 8
HALF = NODES // 2
RATE_LOW, RATE_HIGH = 3.66e-5, 0.0333334
TILE = 1024
VMEM_MIB = 44
BF = jnp.bfloat16
F32 = jnp.float32


def cheb(low, high):
    k = np.arange(NODES)
    x = np.cos(np.pi * (2 * k + 1) / (2 * NODES))
    return 0.5 * (low + high) + 0.5 * (high - low) * x


def cardinal(nodes, points):
    rates = cheb(RATE_LOW, RATE_HIGH)
    points = np.asarray(points, np.float64)
    left = np.exp(-np.outer(rates, nodes)).astype(np.longdouble)
    right = np.exp(-np.outer(rates, points.ravel())).astype(np.longdouble)
    for i in range(len(nodes)):
        pivot = i + int(np.argmax(np.abs(left[i:, i])))
        left[[i, pivot]], right[[i, pivot]] = left[[pivot, i]], right[[pivot, i]]
        right[i] /= left[i, i]
        left[i] /= left[i, i]
        for k in range(len(nodes)):
            if k != i:
                right[k] -= left[k, i] * right[i]
                left[k] -= left[k, i] * left[i]
    return right.astype(np.float64).reshape((len(nodes),) + points.shape)


def split_pair(matrix):
    high = matrix.astype(jnp.bfloat16)
    low = (matrix - high.astype(np.float64)).astype(jnp.bfloat16)
    return np.concatenate([high, low], axis=1)


def constants(rows):
    source = cheb(0.0, rows - 1.0)
    target = cheb(0.0, rows + SHORT - 2.0)
    lags = cheb(2.0 - SHORT, rows - 1.0)
    moment = np.zeros((16, rows))
    basis = cardinal(source, np.arange(rows))
    moment[:HALF] = basis[:HALF]
    moment[8 : 8 + HALF] = basis[HALF:]
    spread = np.zeros((rows + 8, NODES))
    spread[: rows + SHORT - 1] = cardinal(target, np.arange(rows + SHORT - 1)).T
    place = np.arange(rows)
    lag = place[None, :] - place[:, None]
    inside = cardinal(lags, lag) * (lag >= 0)[None]
    place = np.arange(16)
    lag = place[None, :] - place[:8, None]
    live = (lag < 0) & (place[:8, None] < SHORT - 1)
    beyond = -cardinal(lags, np.where(live, lag, 0)) * live[None]
    wide = np.zeros((NODES * 8 + 16 + rows + 8, 2 * rows), jnp.bfloat16)
    wide[: NODES * 8, :32] = split_pair(beyond.reshape(NODES * 8, 16))
    wide[NODES * 8 : NODES * 8 + 16] = split_pair(moment)
    wide[NODES * 8 + 16 :, : 2 * NODES] = split_pair(spread)
    matrices = np.concatenate([split_pair(inside.reshape(NODES * rows, rows)), wide], axis=0)
    return source, rows - target, lags, matrices


def doubled(x):
    return jnp.concatenate([x, x], axis=1)


def low_lanes():
    return lax.broadcasted_iota(jnp.int32, (8, 128), 1) < 64


def top_rows():
    return lax.broadcasted_iota(jnp.int32, (8, 128), 0) < HALF


def packed_rows(values):
    row = lax.broadcasted_iota(jnp.int32, (8, 128), 0) % HALF
    low = low_lanes()
    out = jnp.zeros((8, 128), F32)
    for r in range(HALF):
        out = jnp.where(row == r, jnp.where(low, F32(values[r]), F32(values[r + HALF])), out)
    return out


def unpack(first, second, low):
    return (
        jnp.where(low, first, pltpu.roll(second, 64, 1)),
        jnp.where(low, pltpu.roll(first, 64, 1), second),
    )


def filter_nodes(rate, res, lags):
    rate, res = doubled(rate), doubled(res)
    place = packed_rows(lags)
    total = jnp.zeros((8, 128), F32)
    for m in range(MODES):
        total = total + res[m : m + 1] * jnp.exp(-rate[m : m + 1] * place)
    return total


def twice(x):
    return jnp.concatenate([x, x], axis=0)


class Rows:
    def __init__(self, rows):
        self.inside = slice(0, NODES * rows)
        self.beyond = slice(NODES * rows, NODES * rows + NODES * 8)
        self.moment = slice(self.beyond.stop, self.beyond.stop + 16)
        self.spread = slice(self.moment.stop, self.moment.stop + rows + 8)


def send_moments(product, matrix, taps, at, pay_ref):
    low, top = low_lanes(), top_rows()
    moments = jnp.dot(matrix, twice(product), preferred_element_type=F32)
    blocks = []
    for t in range(product.shape[1] // 128):
        columns = slice(t * 128, t * 128 + 128)
        first, second = unpack(moments[0:8, columns], moments[8:16, columns], low)
        if taps is None:
            blocks.append(jnp.where(top, first, pltpu.roll(second, HALF, 0)))
        else:
            blocks += [jnp.where(top, first, taps), jnp.where(top, second, taps)]
    for k in range(0, len(blocks), 2):
        start = at // 64 * 8 // (2 if taps is None else 1) + k * 8
        pay_ref[start : start + 16, :] = jnp.concatenate(blocks[k : k + 2], axis=0).astype(BF)


def tiles(channels):
    return [(at, slice(at, at + TILE)) for at in range(0, channels, TILE)]


def first_kernel(lags, g_ref, gate_ref, rate_ref, res_ref, moment_ref, pay_ref, halo_ref, next_ref, late_ref):
    next_ref[...] = jnp.concatenate([rate_ref[1], res_ref[1]], axis=0)
    taps = filter_nodes(rate_ref[0], res_ref[0], lags)
    matrix = moment_ref[...]
    for at, cut in tiles(g_ref.shape[1]):
        product = (gate_ref[0, :, cut].astype(F32) * g_ref[:, cut].astype(F32)).astype(BF)
        halo_ref[:, cut] = product[:16]
        late_ref[:, cut] = gate_ref[1, :, cut]
        send_moments(product, matrix, taps, at, pay_ref)


def scan_body(source, gaps, rows, rate, res, pay_ref, out_ref, taps):
    low, top = low_lanes(), top_rows()
    width = HALF if taps is None else 2 * HALF
    groups = pay_ref.shape[0] // 16
    rate, res = doubled(rate), doubled(res)
    enter = []
    for r in range(HALF):
        place = jnp.where(low, F32(source[r]), F32(source[r + HALF]))
        enter.append([jnp.exp(-rate[8 * o : 8 * o + 8] * place) for o in range(2)])
    step = [jnp.exp(-rate[8 * o : 8 * o + 8] * F32(rows)) for o in range(2)]
    gap = packed_rows(gaps)
    leave = [res[m : m + 1] * jnp.exp(-rate[m : m + 1] * gap) for m in range(MODES)]

    def one(block, state):
        total = jnp.zeros((8, 128), F32)
        for m in range(MODES):
            total = total + leave[m] * state[m // 8][m % 8 : m % 8 + 1]
        sums = [None, None]
        for o in range(2):
            part = enter[0][o] * block[0:1]
            for r in range(1, HALF):
                part = part + enter[r][o] * block[r : r + 1]
            sums[o] = part + pltpu.roll(part, 64, 1)
        return total, tuple(step[o] * state[o] + sums[o] for o in range(2))

    def several(i, state):
        place = pl.ds(pl.multiple_of((groups - 1 - i) * 16, 16), 16)
        blocks = pay_ref[place, :].astype(F32)
        outs = [None] * (16 // width)
        for k in reversed(range(len(outs))):
            outs[k], state = one(blocks[k * width : k * width + HALF], state)
        if taps is None:
            outs = [jnp.where(top, outs[k], outs[k + 1]) for k in range(0, len(outs), 2)]
        else:
            outs = [jnp.where(top, out, taps) for out in outs]
        out_ref[place, :] = jnp.concatenate(outs, axis=0).astype(BF)
        return state

    zero = jnp.zeros((8, 128), F32)
    lax.fori_loop(0, groups, several, (zero, zero), unroll=4 if width == 8 else 2)


def scan_first_kernel(source, gaps, lags, rows, pay_ref, rate_ref, res_ref, next_ref, out_ref):
    taps = filter_nodes(next_ref[:MODES], next_ref[MODES:], lags)
    scan_body(source, gaps, rows, rate_ref[0], res_ref[0], pay_ref, out_ref, taps)


def scan_last_kernel(source, gaps, rows, pay_ref, next_ref, out_ref):
    scan_body(source, gaps, rows, next_ref[:MODES], next_ref[MODES:], pay_ref, out_ref, None)


def inside_kernel(g_ref, gate_ref, halo_ref, pay_ref, matrix_ref, local_ref, rim_ref):
    rows, channels = g_ref.shape
    where = Rows(rows)
    low = low_lanes()
    for at, cut in tiles(channels):
        gate = gate_ref[0, :, cut] if len(gate_ref.shape) == 3 else gate_ref[:, cut]
        product = (gate.astype(F32) * g_ref[:, cut].astype(F32)).astype(BF)
        parts = []
        for t in range(at // 128, (at + TILE) // 128):
            both = pay_ref[t * 16 : t * 16 + 16, :].astype(F32)
            parts.append(unpack(both[:8], both[8:], low))
        taps = [jnp.concatenate([part[h] for part in parts], axis=1) for h in range(2)]
        waves = jnp.dot(matrix_ref[where.inside, :], twice(product), preferred_element_type=F32)
        edges = jnp.dot(matrix_ref[where.beyond, :32], twice(halo_ref[:, cut]), preferred_element_type=F32)
        local = None
        rim = None
        for n in range(NODES):
            tap = taps[n // HALF][HALF + n % HALF : HALF + n % HALF + 1]
            wave = tap * waves[n * rows : (n + 1) * rows]
            edge = tap * edges[n * 8 : (n + 1) * 8]
            local = wave if local is None else local + wave
            rim = edge if rim is None else rim + edge
        local_ref[:, cut] = local
        rim_ref[:, cut] = rim


class Fetch:
    def __init__(self, far, near, sems):
        self.near = near
        self.copies = [
            pltpu.make_async_copy(far.at[:, cut], near.at[:, cut], sems.at[k])
            for k, (_, cut) in enumerate(tiles(near.shape[1]))
        ]

    def start(self, at):
        self.copies[at // TILE].start()

    def tile(self, at):
        self.copies[at // TILE].wait()
        return self.near[:, at : at + TILE].astype(F32)


def updated_tile(at, cut, g, local_ref, rim_ref, pay_ref, matrix, short):
    rows, channels = g.near.shape
    low, top = low_lanes(), top_rows()
    parts = []
    for t in range(at // 128, (at + TILE) // 128):
        if pay_ref.shape[0] * 8 == channels:
            both = pay_ref[t * 16 : t * 16 + 16, :].astype(F32)
            first, second = unpack(both[:8], both[8:], low)
        else:
            both = pay_ref[t // 2 * 16 : t // 2 * 16 + 16, :].astype(F32)[t % 2 * 8 : t % 2 * 8 + 8]
            first, second = unpack(both, pltpu.roll(both, HALF, 0), low)
        parts.append(jnp.where(top, first, pltpu.roll(second, HALF, 0)))
    nodes = jnp.concatenate(parts, axis=1).astype(BF)
    nodes = jnp.concatenate([nodes, nodes], axis=0)
    outside = jnp.dot(matrix, nodes, preferred_element_type=F32)
    carried = (local_ref[:, cut] + outside[:rows]).astype(BF).astype(F32)
    rim = (rim_ref[:, cut] + outside[rows:]).astype(BF).astype(F32)
    extended = jnp.concatenate([carried, rim], axis=0)
    tail = None
    for j in range(SHORT):
        term = short[j : j + 1] * extended[j : j + rows]
        tail = term if tail is None else tail + term
    return (g.tile(at) + tail).astype(BF)


def turn_kernel(
    g_far, local_ref, rim_ref, nodes_ref, short_ref, gate_far, matrix_ref, gate_late, short_late,
    new_far, pay_ref, halo_ref, g_near, gate_near, new_near, g_sem, gate_sem, new_sem,
):
    where = Rows(g_near.shape[0])
    g, gate = Fetch(g_far, g_near, g_sem), Fetch(gate_far, gate_near, gate_sem)
    out = Fetch(new_near, new_far, new_sem)
    for at, _ in tiles(g_near.shape[1]):
        g.start(at)
        gate.start(at)
    spread = matrix_ref[where.spread, : 2 * NODES]
    moment = matrix_ref[where.moment, :]
    for at, cut in tiles(g_near.shape[1]):
        new = updated_tile(at, cut, g, local_ref, rim_ref, nodes_ref, spread, short_ref[0, :, cut])
        new_near[:, cut] = new
        out.start(at)
        product = (gate.tile(at) * new.astype(F32)).astype(BF)
        halo_ref[:, cut] = product[:16]
        send_moments(product, moment, None, at, pay_ref)
    for copy in out.copies:
        copy.wait()


def order_kernel(nodes_ref, rim_ref, out_ref):
    out_ref[...] = nodes_ref[...]


def last_kernel(
    g_far, local_ref, rim_ref, nodes_ref, short_ref, matrix_ref, out_far, g_near, out_near, g_sem, out_sem
):
    spread = matrix_ref[Rows(g_near.shape[0]).spread, : 2 * NODES]
    g, out = Fetch(g_far, g_near, g_sem), Fetch(out_near, out_far, out_sem)
    for at, _ in tiles(g_near.shape[1]):
        g.start(at)
    for at, cut in tiles(g_near.shape[1]):
        out_near[:, cut] = updated_tile(at, cut, g, local_ref, rim_ref, nodes_ref, spread, short_ref[:, cut])
        out.start(at)
    for copy in out.copies:
        copy.wait()


PARAMS = pltpu.CompilerParams(vmem_limit_bytes=VMEM_MIB * 1024 * 1024)


def call(kernel, name, ins, outs, fixed=(), specs=None, out_specs=None, flops=0, scratch=None):
    def whole(array):
        if scratch:
            return pl.BlockSpec(memory_space=pltpu.VMEM)
        return pl.BlockSpec(array.shape, lambda i: (0,) * len(array.shape))

    return pl.pallas_call(
        lambda *refs: kernel(*fixed, *refs),
        **({"scratch_shapes": scratch} if scratch else {"grid": (1,)}),
        in_specs=[(specs or {}).get(k) or whole(x) for k, x in enumerate(ins)],
        out_specs=[(out_specs or {}).get(k) or whole(x) for k, x in enumerate(outs)],
        out_shape=list(outs),
        compiler_params=PARAMS,
        cost_estimate=pl.CostEstimate(flops=flops, bytes_accessed=8 * 2**20, transcendentals=0),
        name=name,
    )(*ins)


def in_hbm(x):
    return pltpu.with_memory_space_constraint(x, pltpu.HBM)


def on_device(cotangent, gates, short_weight, decay_rates, residues):
    g = in_hbm(cotangent[0])
    gates = in_hbm(gates[0])
    short_weight = short_weight[0]
    rates = in_hbm(jnp.swapaxes(decay_rates[0], 1, 2))
    weights = in_hbm(jnp.swapaxes(residues[0], 1, 2))
    rows, channels = g.shape
    shards = lax.axis_size("seq")
    segments = lax.axis_size("segment")
    source, gaps, lags, matrices = constants(rows)
    moment = in_hbm(jnp.asarray(matrices[Rows(rows).moment]))
    matrices = jnp.asarray(matrices)

    def shape(size, dtype):
        return jax.ShapeDtypeStruct(size, dtype)

    def around(x, distance):
        return lax.ppermute(x, "segment", [(i, (i + distance) % segments) for i in range(segments)])

    def across(x):
        blocks = x.reshape(shards, x.shape[0] // shards, 128)
        return lax.all_to_all(blocks, "seq", split_axis=0, concat_axis=0, tiled=True).reshape(x.shape)

    pay_shape = shape((shards * 2 * HALF, 128), BF)
    short_pay_shape = shape((shards * HALF, 128), BF)
    halo_shape = shape((16, channels), BF)
    row_shape = shape((rows, channels), BF)
    local_shapes = [shape((rows, channels), F32), shape((8, channels), F32)]
    layer_gate = pl.BlockSpec((1, rows, channels), lambda i: (0, 0, 0))

    pay, halo, params, late_gates = call(
        first_kernel, "first", [g, gates, rates, weights, moment],
        [pay_shape, halo_shape, shape((2 * MODES, channels // shards), F32), row_shape],
        fixed=(lags,),
    )
    gates_early = in_hbm(around(late_gates, 1))
    gates_late = in_hbm(around(late_gates, -1))
    params_late = around(params, -1)
    params_early = around(params, 1)
    short_late = around(short_weight[1], -1)
    halo = lax.ppermute(halo, "seq", [(i, i - 1) for i in range(1, shards)])
    got = across(pay)
    (back,) = call(
        scan_first_kernel, "scan", [got, rates, weights, params_late], [pay_shape], fixed=(source, gaps, lags, rows)
    )
    nodes = across(back)
    local, rim = call(
        inside_kernel, "inside", [g, gates, halo, got, matrices], local_shapes, specs={1: layer_gate},
        flops=2 * NODES * rows * 2 * rows * channels,
    )
    taps = nodes
    anywhere = pl.BlockSpec(memory_space=pl.ANY)
    near = [pltpu.VMEM((rows, channels), BF)]
    sems = [pltpu.SemaphoreType.DMA((channels // TILE,))]
    g, pay, halo = call(
        turn_kernel, "turn", [g, local, rim, nodes, short_weight, gates_early, matrices, gates_late, short_late],
        [row_shape, short_pay_shape, halo_shape],
        specs={0: anywhere, 5: anywhere, 7: anywhere, 8: anywhere}, out_specs={0: anywhere},
        scratch=near * 3 + sems * 3,
    )
    moves = [
        (s * shards + k, (s - 2) % segments * shards + k - 1) for s in range(segments) for k in range(1, shards)
    ]
    halo = lax.ppermute(halo, ("segment", "seq"), moves)
    g = in_hbm(around(g, -2))
    got = across(pay)
    (back,) = call(
        scan_last_kernel, "scan", [got, params_early], [short_pay_shape], fixed=(source, gaps, rows)
    )
    nodes = across(back)
    local, rim = call(
        inside_kernel, "inside", [g, gates_late, halo, taps, matrices], local_shapes,
        flops=2 * NODES * rows * 2 * rows * channels,
    )
    nodes = pl.pallas_call(
        order_kernel,
        in_specs=[pl.BlockSpec(memory_space=pltpu.VMEM), anywhere],
        out_specs=pl.BlockSpec(memory_space=pltpu.VMEM),
        out_shape=short_pay_shape,
        compiler_params=PARAMS,
        name="order",
    )(nodes, rim)
    nodes = around(nodes, -2)
    (g,) = call(
        last_kernel, "last", [g, local, rim, nodes, short_late, matrices], [row_shape],
        specs={0: anywhere}, out_specs={0: anywhere}, scratch=near * 2 + sems * 2,
    )
    return g[None]


def solution(mesh):
    in_specs = (
        P("segment", "seq", None),
        P("segment", None, "seq", None),
        P("segment", None, None, None),
        P("segment", None, "seq", None),
        P("segment", None, "seq", None),
    )
    return jax.shard_map(
        on_device, mesh=mesh, in_specs=in_specs, out_specs=P("segment", "seq", None), check_vma=False
    )
```

```python
import jax
import jax.numpy as jnp
import numpy as np
from jax import lax
from jax.experimental import pallas as pl
from jax.experimental.pallas import tpu as pltpu
from jax.sharding import PartitionSpec as P

MODES = 16
SHORT = 7
NODES = 8
HALF = NODES // 2
RATE_LOW, RATE_HIGH = 3.66e-5, 0.0333334
TILE = 2048
VMEM_MIB = 44
BF = jnp.bfloat16
F32 = jnp.float32


def cheb(low, high):
    k = np.arange(NODES)
    x = np.cos(np.pi * (2 * k + 1) / (2 * NODES))
    return 0.5 * (low + high) + 0.5 * (high - low) * x


def cardinal(nodes, points):
    rates = cheb(RATE_LOW, RATE_HIGH)
    points = np.asarray(points, np.float64)
    left = np.exp(-np.outer(rates, nodes)).astype(np.longdouble)
    right = np.exp(-np.outer(rates, points.ravel())).astype(np.longdouble)
    for i in range(len(nodes)):
        pivot = i + int(np.argmax(np.abs(left[i:, i])))
        left[[i, pivot]], right[[i, pivot]] = left[[pivot, i]], right[[pivot, i]]
        right[i] /= left[i, i]
        left[i] /= left[i, i]
        for k in range(len(nodes)):
            if k != i:
                right[k] -= left[k, i] * right[i]
                left[k] -= left[k, i] * left[i]
    return right.astype(np.float64).reshape((len(nodes),) + points.shape)


def split_pair(matrix):
    high = matrix.astype(jnp.bfloat16)
    low = (matrix - high.astype(np.float64)).astype(jnp.bfloat16)
    return np.concatenate([high, low], axis=1)


def constants(rows):
    source = cheb(0.0, rows - 1.0)
    target = cheb(0.0, rows + SHORT - 2.0)
    lags = cheb(2.0 - SHORT, rows - 1.0)
    moment = np.zeros((16, rows))
    basis = cardinal(source, np.arange(rows))
    moment[:HALF] = basis[:HALF]
    moment[8 : 8 + HALF] = basis[HALF:]
    spread = np.zeros((rows + 8, NODES))
    spread[: rows + SHORT - 1] = cardinal(target, np.arange(rows + SHORT - 1)).T
    place = np.arange(rows)
    lag = place[None, :] - place[:, None]
    inside = cardinal(lags, lag) * (lag >= 0)[None]
    place = np.arange(16)
    lag = place[None, :] - place[:8, None]
    live = (lag < 0) & (place[:8, None] < SHORT - 1)
    beyond = -cardinal(lags, np.where(live, lag, 0)) * live[None]
    wide = np.zeros((NODES * 8 + 16 + rows + 8, 2 * rows), jnp.bfloat16)
    wide[: NODES * 8, :32] = split_pair(beyond.reshape(NODES * 8, 16))
    wide[NODES * 8 : NODES * 8 + 16] = split_pair(moment)
    wide[NODES * 8 + 16 :, : 2 * NODES] = split_pair(spread)
    matrices = np.concatenate([split_pair(inside.reshape(NODES * rows, rows)), wide], axis=0)
    return source, rows - target, lags, matrices


def doubled(x):
    return jnp.concatenate([x, x], axis=1)


def low_lanes():
    return lax.broadcasted_iota(jnp.int32, (8, 128), 1) < 64


def top_rows():
    return lax.broadcasted_iota(jnp.int32, (8, 128), 0) < HALF


def packed_rows(values):
    row = lax.broadcasted_iota(jnp.int32, (8, 128), 0) % HALF
    low = low_lanes()
    out = jnp.zeros((8, 128), F32)
    for r in range(HALF):
        out = jnp.where(row == r, jnp.where(low, F32(values[r]), F32(values[r + HALF])), out)
    return out


def unpack(first, second, low):
    return (
        jnp.where(low, first, pltpu.roll(second, 64, 1)),
        jnp.where(low, pltpu.roll(first, 64, 1), second),
    )


def filter_nodes(rate, res, lags):
    rate, res = doubled(rate), doubled(res)
    place = packed_rows(lags)
    total = jnp.zeros((8, 128), F32)
    for m in range(MODES):
        total = total + res[m : m + 1] * jnp.exp(-rate[m : m + 1] * place)
    return total


def twice(x):
    return jnp.concatenate([x, x], axis=0)


class Rows:
    def __init__(self, rows):
        self.inside = slice(0, NODES * rows)
        self.beyond = slice(NODES * rows, NODES * rows + NODES * 8)
        self.moment = slice(self.beyond.stop, self.beyond.stop + 16)
        self.spread = slice(self.moment.stop, self.moment.stop + rows + 8)


def send_moments(product, matrix, taps, at, pay_ref):
    low, top = low_lanes(), top_rows()
    moments = jnp.dot(matrix, twice(product), preferred_element_type=F32)
    blocks = []
    for t in range(product.shape[1] // 128):
        columns = slice(t * 128, t * 128 + 128)
        first, second = unpack(moments[0:8, columns], moments[8:16, columns], low)
        if taps is None:
            blocks.append(jnp.where(top, first, pltpu.roll(second, HALF, 0)))
        else:
            blocks += [jnp.where(top, first, taps), jnp.where(top, second, taps)]
    for k in range(0, len(blocks), 2):
        start = at // 64 * 8 // (2 if taps is None else 1) + k * 8
        pay_ref[start : start + 16, :] = jnp.concatenate(blocks[k : k + 2], axis=0).astype(BF)


def tiles(channels):
    return [(at, slice(at, at + TILE)) for at in range(0, channels, TILE)]


def first_kernel(lags, g_ref, gate_ref, rate_ref, res_ref, moment_ref, pay_ref, halo_ref, next_ref, late_ref):
    next_ref[...] = jnp.concatenate([rate_ref[1], res_ref[1]], axis=0)
    taps = filter_nodes(rate_ref[0], res_ref[0], lags)
    matrix = moment_ref[...]
    for at, cut in tiles(g_ref.shape[1]):
        product = (gate_ref[0, :, cut].astype(F32) * g_ref[:, cut].astype(F32)).astype(BF)
        halo_ref[:, cut] = product[:16]
        late_ref[:, cut] = gate_ref[1, :, cut]
        send_moments(product, matrix, taps, at, pay_ref)


def scan_body(source, gaps, rows, rate, res, pay_ref, out_ref, taps):
    low, top = low_lanes(), top_rows()
    width = HALF if taps is None else 2 * HALF
    groups = pay_ref.shape[0] // 16
    rate, res = doubled(rate), doubled(res)
    enter = []
    for r in range(HALF):
        place = jnp.where(low, F32(source[r]), F32(source[r + HALF]))
        enter.append([jnp.exp(-rate[8 * o : 8 * o + 8] * place) for o in range(2)])
    step = [jnp.exp(-rate[8 * o : 8 * o + 8] * F32(rows)) for o in range(2)]
    gap = packed_rows(gaps)
    leave = [res[m : m + 1] * jnp.exp(-rate[m : m + 1] * gap) for m in range(MODES)]

    def one(block, state):
        total = jnp.zeros((8, 128), F32)
        for m in range(MODES):
            total = total + leave[m] * state[m // 8][m % 8 : m % 8 + 1]
        sums = [None, None]
        for o in range(2):
            part = enter[0][o] * block[0:1]
            for r in range(1, HALF):
                part = part + enter[r][o] * block[r : r + 1]
            sums[o] = part + pltpu.roll(part, 64, 1)
        return total, tuple(step[o] * state[o] + sums[o] for o in range(2))

    def several(i, state):
        place = pl.ds(pl.multiple_of((groups - 1 - i) * 16, 16), 16)
        blocks = pay_ref[place, :].astype(F32)
        outs = [None] * (16 // width)
        for k in reversed(range(len(outs))):
            outs[k], state = one(blocks[k * width : k * width + HALF], state)
        if taps is None:
            outs = [jnp.where(top, outs[k], outs[k + 1]) for k in range(0, len(outs), 2)]
        else:
            outs = [jnp.where(top, out, taps) for out in outs]
        out_ref[place, :] = jnp.concatenate(outs, axis=0).astype(BF)
        return state

    zero = jnp.zeros((8, 128), F32)
    lax.fori_loop(0, groups, several, (zero, zero), unroll=4 if width == 8 else 2)


def scan_first_kernel(source, gaps, lags, rows, pay_ref, rate_ref, res_ref, next_ref, out_ref):
    taps = filter_nodes(next_ref[:MODES], next_ref[MODES:], lags)
    scan_body(source, gaps, rows, rate_ref[0], res_ref[0], pay_ref, out_ref, taps)


def scan_last_kernel(source, gaps, rows, pay_ref, next_ref, out_ref):
    scan_body(source, gaps, rows, next_ref[:MODES], next_ref[MODES:], pay_ref, out_ref, None)


def inside_kernel(g_ref, gate_ref, halo_ref, pay_ref, matrix_ref, local_ref, rim_ref):
    rows, channels = g_ref.shape
    where = Rows(rows)
    low = low_lanes()
    for at, cut in tiles(channels):
        gate = gate_ref[0, :, cut] if len(gate_ref.shape) == 3 else gate_ref[:, cut]
        product = (gate.astype(F32) * g_ref[:, cut].astype(F32)).astype(BF)
        parts = []
        for t in range(at // 128, (at + TILE) // 128):
            both = pay_ref[t * 16 : t * 16 + 16, :].astype(F32)
            parts.append(unpack(both[:8], both[8:], low))
        taps = [jnp.concatenate([part[h] for part in parts], axis=1) for h in range(2)]
        waves = jnp.dot(matrix_ref[where.inside, :], twice(product), preferred_element_type=F32)
        edges = jnp.dot(matrix_ref[where.beyond, :32], twice(halo_ref[:, cut]), preferred_element_type=F32)
        local = None
        rim = None
        for n in range(NODES):
            tap = taps[n // HALF][HALF + n % HALF : HALF + n % HALF + 1]
            wave = tap * waves[n * rows : (n + 1) * rows]
            edge = tap * edges[n * 8 : (n + 1) * 8]
            local = wave if local is None else local + wave
            rim = edge if rim is None else rim + edge
        local_ref[:, cut] = local
        rim_ref[:, cut] = rim


class Fetch:
    def __init__(self, far, near, sems):
        self.near = near
        self.copies = [
            pltpu.make_async_copy(far.at[:, cut], near.at[:, cut], sems.at[k])
            for k, (_, cut) in enumerate(tiles(near.shape[1]))
        ]

    def start(self, at):
        self.copies[at // TILE].start()

    def tile(self, at):
        self.copies[at // TILE].wait()
        return self.near[:, at : at + TILE].astype(F32)


def updated_tile(at, cut, g, local_ref, rim_ref, pay_ref, matrix, short):
    rows, channels = g.near.shape
    low, top = low_lanes(), top_rows()
    parts = []
    for t in range(at // 128, (at + TILE) // 128):
        if pay_ref.shape[0] * 8 == channels:
            both = pay_ref[t * 16 : t * 16 + 16, :].astype(F32)
            first, second = unpack(both[:8], both[8:], low)
        else:
            both = pay_ref[t // 2 * 16 : t // 2 * 16 + 16, :].astype(F32)[t % 2 * 8 : t % 2 * 8 + 8]
            first, second = unpack(both, pltpu.roll(both, HALF, 0), low)
        parts.append(jnp.where(top, first, pltpu.roll(second, HALF, 0)))
    nodes = jnp.concatenate(parts, axis=1).astype(BF)
    nodes = jnp.concatenate([nodes, nodes], axis=0)
    outside = jnp.dot(matrix, nodes, preferred_element_type=F32)
    carried = (local_ref[:, cut] + outside[:rows]).astype(BF).astype(F32)
    rim = (rim_ref[:, cut] + outside[rows:]).astype(BF).astype(F32)
    extended = jnp.concatenate([carried, rim], axis=0)
    tail = None
    for j in range(SHORT):
        term = short[j : j + 1] * extended[j : j + rows]
        tail = term if tail is None else tail + term
    return (g.tile(at) + tail).astype(BF)


def turn_kernel(
    g_far, local_ref, rim_ref, nodes_ref, short_ref, gate_far, matrix_ref, gate_late, short_late,
    new_far, pay_ref, halo_ref, g_near, gate_near, new_near, g_sem, gate_sem, new_sem,
):
    where = Rows(g_near.shape[0])
    g, gate = Fetch(g_far, g_near, g_sem), Fetch(gate_far, gate_near, gate_sem)
    out = Fetch(new_near, new_far, new_sem)
    for at, _ in tiles(g_near.shape[1]):
        g.start(at)
        gate.start(at)
    spread = matrix_ref[where.spread, : 2 * NODES]
    moment = matrix_ref[where.moment, :]
    for at, cut in tiles(g_near.shape[1]):
        new = updated_tile(at, cut, g, local_ref, rim_ref, nodes_ref, spread, short_ref[0, :, cut])
        new_near[:, cut] = new
        out.start(at)
        product = (gate.tile(at) * new.astype(F32)).astype(BF)
        halo_ref[:, cut] = product[:16]
        send_moments(product, moment, None, at, pay_ref)
    for copy in out.copies:
        copy.wait()


def order_kernel(nodes_ref, rim_ref, out_ref):
    out_ref[...] = nodes_ref[...]


def last_kernel(
    g_far, local_ref, rim_ref, nodes_ref, short_ref, matrix_ref, out_far, g_near, out_near, g_sem, out_sem
):
    spread = matrix_ref[Rows(g_near.shape[0]).spread, : 2 * NODES]
    g, out = Fetch(g_far, g_near, g_sem), Fetch(out_near, out_far, out_sem)
    for at, _ in tiles(g_near.shape[1]):
        g.start(at)
    for at, cut in tiles(g_near.shape[1]):
        out_near[:, cut] = updated_tile(at, cut, g, local_ref, rim_ref, nodes_ref, spread, short_ref[:, cut])
        out.start(at)
    for copy in out.copies:
        copy.wait()


PARAMS = pltpu.CompilerParams(vmem_limit_bytes=VMEM_MIB * 1024 * 1024)


def call(kernel, name, ins, outs, fixed=(), specs=None, out_specs=None, flops=0, scratch=None):
    def whole(array):
        if scratch:
            return pl.BlockSpec(memory_space=pltpu.VMEM)
        return pl.BlockSpec(array.shape, lambda i: (0,) * len(array.shape))

    return pl.pallas_call(
        lambda *refs: kernel(*fixed, *refs),
        **({"scratch_shapes": scratch} if scratch else {"grid": (1,)}),
        in_specs=[(specs or {}).get(k) or whole(x) for k, x in enumerate(ins)],
        out_specs=[(out_specs or {}).get(k) or whole(x) for k, x in enumerate(outs)],
        out_shape=list(outs),
        compiler_params=PARAMS,
        cost_estimate=pl.CostEstimate(flops=flops, bytes_accessed=8 * 2**20, transcendentals=0),
        name=name,
    )(*ins)


def in_hbm(x):
    return pltpu.with_memory_space_constraint(x, pltpu.HBM)


def on_device(cotangent, gates, short_weight, decay_rates, residues):
    g = in_hbm(cotangent[0])
    gates = in_hbm(gates[0])
    short_weight = short_weight[0]
    rates = in_hbm(jnp.swapaxes(decay_rates[0], 1, 2))
    weights = in_hbm(jnp.swapaxes(residues[0], 1, 2))
    rows, channels = g.shape
    shards = lax.axis_size("seq")
    segments = lax.axis_size("segment")
    source, gaps, lags, matrices = constants(rows)
    moment = in_hbm(jnp.asarray(matrices[Rows(rows).moment]))
    matrices = jnp.asarray(matrices)

    def shape(size, dtype):
        return jax.ShapeDtypeStruct(size, dtype)

    def around(x, distance):
        return lax.ppermute(x, "segment", [(i, (i + distance) % segments) for i in range(segments)])

    def across(x):
        blocks = x.reshape(shards, x.shape[0] // shards, 128)
        return lax.all_to_all(blocks, "seq", split_axis=0, concat_axis=0, tiled=True).reshape(x.shape)

    pay_shape = shape((shards * 2 * HALF, 128), BF)
    short_pay_shape = shape((shards * HALF, 128), BF)
    halo_shape = shape((16, channels), BF)
    row_shape = shape((rows, channels), BF)
    local_shapes = [shape((rows, channels), F32), shape((8, channels), F32)]
    layer_gate = pl.BlockSpec((1, rows, channels), lambda i: (0, 0, 0))

    pay, halo, params, late_gates = call(
        first_kernel, "first", [g, gates, rates, weights, moment],
        [pay_shape, halo_shape, shape((2 * MODES, channels // shards), F32), row_shape],
        fixed=(lags,),
    )
    gates_early = in_hbm(around(late_gates, 1))
    gates_late = in_hbm(around(late_gates, -1))
    params_late = around(params, -1)
    params_early = around(params, 1)
    short_late = around(short_weight[1], -1)
    halo = lax.ppermute(halo, "seq", [(i, i - 1) for i in range(1, shards)])
    got = across(pay)
    (back,) = call(
        scan_first_kernel, "scan", [got, rates, weights, params_late], [pay_shape], fixed=(source, gaps, lags, rows)
    )
    nodes = across(back)
    local, rim = call(
        inside_kernel, "inside", [g, gates, halo, got, matrices], local_shapes, specs={1: layer_gate},
        flops=2 * NODES * rows * 2 * rows * channels,
    )
    taps = nodes
    anywhere = pl.BlockSpec(memory_space=pl.ANY)
    near = [pltpu.VMEM((rows, channels), BF)]
    sems = [pltpu.SemaphoreType.DMA((channels // TILE,))]
    g, pay, halo = call(
        turn_kernel, "turn", [g, local, rim, nodes, short_weight, gates_early, matrices, gates_late, short_late],
        [row_shape, short_pay_shape, halo_shape],
        specs={0: anywhere, 5: anywhere, 7: anywhere, 8: anywhere}, out_specs={0: anywhere},
        scratch=near * 3 + sems * 3,
    )
    moves = [
        (s * shards + k, (s - 2) % segments * shards + k - 1) for s in range(segments) for k in range(1, shards)
    ]
    halo = lax.ppermute(halo, ("segment", "seq"), moves)
    g = in_hbm(around(g, -2))
    got = across(pay)
    (back,) = call(
        scan_last_kernel, "scan", [got, params_early], [short_pay_shape], fixed=(source, gaps, rows)
    )
    nodes = across(back)
    local, rim = call(
        inside_kernel, "inside", [g, gates_late, halo, taps, matrices], local_shapes,
        flops=2 * NODES * rows * 2 * rows * channels,
    )
    nodes = pl.pallas_call(
        order_kernel,
        in_specs=[pl.BlockSpec(memory_space=pltpu.VMEM), anywhere],
        out_specs=pl.BlockSpec(memory_space=pltpu.VMEM),
        out_shape=short_pay_shape,
        compiler_params=PARAMS,
        name="order",
    )(nodes, rim)
    nodes = around(nodes, -2)
    (g,) = call(
        last_kernel, "last", [g, local, rim, nodes, short_late, matrices], [row_shape],
        specs={0: anywhere}, out_specs={0: anywhere}, scratch=near * 2 + sems * 2,
    )
    return g[None]


def solution(mesh):
    in_specs = (
        P("segment", "seq", None),
        P("segment", None, "seq", None),
        P("segment", None, None, None),
        P("segment", None, "seq", None),
        P("segment", None, "seq", None),
    )
    return jax.shard_map(
        on_device, mesh=mesh, in_specs=in_specs, out_specs=P("segment", "seq", None), check_vma=False
    )
```
